32 devices in a mesh: section: 4 (over z), row: 4 (over y, x), col: 2 (over core).
Axes of the slice: x: 2, y: 2, z: 4, core: 2. Of those that a mesh axis runs over, the one named last changes fastest.
Arguments:
- act_in: bfloat16 [4, 8, 12288], P('section', 'row', 'col'), may hold values from -6 to 6
- hid_in: bfloat16 [4, 8, 1536], P('section', None, 'row'), may hold values from -6 to 6
- grad_in: bfloat16 [4, 8, 12288], P('section', 'row', 'col'), may hold values from -6 to 6
- saved_in: bfloat16 [4, 8, 12288], P('section', 'row', 'col'), may hold values from -6 to 6
- saved_pre: bfloat16 [4, 8, 1536], P('section', None, 'row'), may hold values from -6 to 6
- weights: bfloat16 [4, 12288, 1536], P('section', 'col', 'row'), may hold values from -0.0546875 to 0.0546875
- norm_gain: float32 [2, 12288], P(None, 'col'), may hold values from 0.25 to 1.75
- norm_bias: float32 [2, 12288], P(None, 'col'), may hold values from -0.5 to 0.5
Outputs:
- act_out: bfloat16 [4, 8, 12288], P('section', 'row', 'col')
- hid_out: bfloat16 [4, 8, 1536], P('section', None, 'row')
- grad_out: bfloat16 [4, 8, 12288], P('section', 'row', 'col')
The draws below stay inside these ranges and needn't reach their ends.
All inputs are finite; a program needn't handle non-finite values.
Results may differ from the reference program's by a relative error of at most 0.0035.
Values may be sent and summed in bfloat16 or wider, within the bound.
A program may use at most 64 MiB of HBM per device.

```python
import jax
import jax.numpy as jnp
from jax import lax

D = 12288
FF = 1536
TOKENS = 8
LAYERS = 2
N_SECTION = 4


def shard_levels(own_key, extent, cuts, least, top_value):
    def one(position, shards_of):
        heights = jax.random.uniform(jax.random.fold_in(jax.random.fold_in(own_key, 6), position), (shards_of,), jnp.float32, least / len(cuts), top_value / len(cuts))
        return jnp.repeat(jnp.exp(heights), extent[position] // shards_of).reshape((-1,) + (1,) * (len(extent) - position - 1))

    level = one(*cuts[0])
    for cut in cuts[1:]:
        level = level * one(*cut)
    return level


def normal_values(own_key, shape, width, limit, pieces=(), held_as=jnp.bfloat16):
    values = jax.random.normal(own_key, shape, jnp.float32) * width
    if len(pieces) > 0:
        values = shard_levels(own_key, shape, pieces, -0.22, 0.18) * values
    return jnp.clip(values, min=-limit, max=limit).astype(held_as)


def setup_inputs(seed: int = 0) -> dict:
    seeds = jax.random.split(jax.random.key(seed), 9)
    act_in = normal_values(seeds[0], (N_SECTION, TOKENS, D), 1.0, 6.0, ((0, 4), (1, 4), (2, 2)))
    hid_in = normal_values(seeds[1], (N_SECTION, TOKENS, FF), 1.0, 6.0, ((0, 4), (2, 4)))
    grad_in = normal_values(seeds[2], (N_SECTION, TOKENS, D), 1.0, 6.0, ((0, 4), (1, 4), (2, 2)))
    saved_in = normal_values(seeds[3], (N_SECTION, TOKENS, D), 1.0, 6.0, ((0, 4), (1, 4), (2, 2)))
    saved_pre = normal_values(seeds[4], (N_SECTION, TOKENS, FF), 1.5, 6.0, ((0, 4), (2, 4)))
    weights = normal_values(seeds[5], (N_SECTION, D, FF), D ** -0.5, 0.0546875, ((0, 4), (1, 2), (2, 4)))
    norm_gain = jnp.clip(1.0 + 0.15 * jax.random.normal(seeds[6], (LAYERS, D), jnp.float32), 0.25, 1.75)
    norm_bias = jnp.clip(jax.random.uniform(seeds[7], (LAYERS, D), jnp.float32, -0.5, 0.5) * shard_levels(seeds[7], (LAYERS, D), ((1, 2),), -0.4, 0.0), -0.5, 0.5)
    return dict(act_in=act_in, hid_in=hid_in, grad_in=grad_in, saved_in=saved_in, saved_pre=saved_pre, weights=weights, norm_gain=norm_gain, norm_bias=norm_bias)


epsilon = 1e-05

def normalized(values):
    floats = values.astype(jnp.float32)
    average = lax.optimization_barrier(jnp.sum(floats, axis=-1, keepdims=True)) / D
    squares = lax.optimization_barrier(jnp.sum(floats * floats, axis=-1, keepdims=True)) / D
    inverse_scale = lax.rsqrt(squares - average * average + epsilon)
    return ((floats - average) * inverse_scale, inverse_scale)

def gelu_slope(preact, upstream):
    return jax.vjp(lambda value: jax.nn.gelu(value, approximate=True), preact)[1](upstream)[0]

def reference(act_in, hid_in, grad_in, saved_in, saved_pre, weights, norm_gain, norm_bias):
    act_list = [None] * N_SECTION
    hid_list = [None] * N_SECTION
    grad_list = [None] * N_SECTION
    for section_index in range(N_SECTION):
        weight = weights[section_index]
        if section_index % 2 == 0:
            layer = section_index // 2
            gain = norm_gain[layer]
            centred, unused_scale = normalized(act_in[section_index])
            normed = (centred * gain + norm_bias[layer]).astype(jnp.bfloat16)
            preact = jnp.dot(normed, weight, preferred_element_type=jnp.float32)
            hidden_out = jax.nn.gelu(preact, approximate=True).astype(jnp.bfloat16)
            forward = act_in[section_index]
            saved_hat, saved_scale = normalized(saved_in[section_index])
            slope = gelu_slope(saved_pre[section_index].astype(jnp.float32), hid_in[section_index].astype(jnp.float32)).astype(jnp.bfloat16)
            back_rows = jnp.dot(slope, weight.T, preferred_element_type=jnp.float32)
            scaled = back_rows * gain
            first_mean = lax.optimization_barrier(jnp.sum(scaled, axis=-1, keepdims=True)) / D
            second_mean = lax.optimization_barrier(jnp.sum(scaled * saved_hat, axis=-1, keepdims=True)) / D
            backward = (grad_in[section_index].astype(jnp.float32) + saved_scale * (scaled - first_mean - saved_hat * second_mean)).astype(jnp.bfloat16)
            hid_list[section_index + 1] = hidden_out
        else:
            term = jnp.dot(hid_in[section_index], weight.T, preferred_element_type=jnp.float32)
            forward = (act_in[section_index].astype(jnp.float32) + term).astype(jnp.bfloat16)
            hidden_out = jnp.dot(grad_in[section_index], weight, preferred_element_type=jnp.float32).astype(jnp.bfloat16)
            backward = grad_in[section_index]
            hid_list[section_index - 1] = hidden_out
        act_list[(section_index + 1) % N_SECTION] = forward
        grad_list[(section_index - 1) % N_SECTION] = backward
    return (jnp.stack(act_list), jnp.stack(hid_list), jnp.stack(grad_list))
```

```python
import functools

import jax
import jax.numpy as jnp
from jax import lax
from jax.experimental import pallas as pl
from jax.experimental.pallas import tpu as pltpu
from jax.sharding import PartitionSpec as P

EPSILON = 1e-05
ROOT = 0.7978845608028654
CUBIC = 0.044715
MESH = pl.DeviceIdType.MESH
LANES = 128


def each(count, body):
    if count <= 8:
        for step in range(count):
            body(step)
    else:
        lax.fori_loop(0, count, lambda step, carry: (body(step), carry)[1], 0)


def gelu(x):
    return x * (0.5 * (1.0 + jnp.tanh(ROOT * (x + CUBIC * (x * x * x)))))


def gelu_slope(x):
    t = jnp.tanh(ROOT * (x + CUBIC * (x * x * x)))
    return 0.5 * (1.0 + t) + 0.5 * x * (1.0 - t * t) * (ROOT * (1.0 + 3.0 * CUBIC * (x * x)))


def row_sum(values):
    return jnp.broadcast_to(jnp.sum(values, axis=-1, keepdims=True), (values.shape[0], LANES))


def kernel(
    sizes,
    act_in, hid_in, grad_in, saved_in, pre_in, weights, gain_in, bias_in,
    act_out, hid_out, grad_out,
    w, lead, other, saved, hid, pre, gain, bias, right, x, mean, scale, stats,
    parts, sums, partial, moments, hidden, result,
    w_sem, local_sem, lead_send, lead_recv, stat_send, stat_recv, part_send, part_recv,
    col_send, col_recv, mom_send, mom_recv, edge_send, edge_recv,
):
    S, R, C, own, T, F, DC, N = sizes
    D = DC * C
    K = DC // N
    s, r, c = lax.axis_index("section"), lax.axis_index("row"), lax.axis_index("col")
    even = s % 2 == 0
    odd = s % 2 == 1
    layer = s // 2
    up, down = (s + 1) % S, (s + S - 1) % S
    me = r * C + c

    def local(src, dst, k):
        return pltpu.make_async_copy(src, dst, local_sem.at[k])

    def remote(src, dst, send, recv, **device):
        return pltpu.make_async_remote_copy(
            src_ref=src, dst_ref=dst, send_sem=send, recv_sem=recv,
            device_id=device, device_id_type=MESH,
        )

    @pl.when(even)
    def _():
        local(act_in.at[0], lead.at[r], 0).start()
        local(grad_in.at[0], other, 1).start()

    @pl.when(odd)
    def _():
        local(grad_in.at[0], lead.at[r], 0).start()
        local(act_in.at[0], other, 1).start()

    rest = [(saved_in.at[0], saved, 2), (hid_in.at[0], hid, 3), (pre_in.at[0], pre, 4)]
    rest += [(gain_in, gain, 5), (bias_in, bias, 6)]
    for item in rest:
        local(*item).start()

    def weight_copy(i):
        rows = pl.ds(i * K, K)
        return pltpu.make_async_copy(weights.at[0, rows], w.at[rows], w_sem.at[i])

    for i in range(N):
        weight_copy(i).start()

    barrier = pltpu.get_barrier_semaphore()
    for neighbour in (up, down):
        pl.semaphore_signal(barrier, inc=1, device_id={"section": neighbour}, device_id_type=MESH)

    def place(k):
        to = (me + k + 1) % (R * C)
        return to, {"row": to // C, "col": to % C}

    def greet(k):
        pl.semaphore_signal(barrier, inc=1, device_id=place(k)[1], device_id_type=MESH)

    each(R * C - 1, greet)

    local(act_in.at[0], lead.at[r], 0).wait()
    local(act_in.at[0], other, 1).wait()
    for item in rest:
        local(*item).wait()

    @pl.when(even)
    def _():
        v = lead[r].astype(jnp.float32)
        z = saved[...].astype(jnp.float32)
        stats[me, 0] = row_sum(v)
        stats[me, 1] = row_sum(v * v)
        stats[me, 2] = row_sum(z)
        stats[me, 3] = row_sum(z * z)

    pl.semaphore_wait(barrier, R * C + 1)

    def lead_copy(to):
        return remote(lead.at[r], lead.at[r], lead_send.at[to], lead_recv.at[r], row=to)

    each(R - 1, lambda k: lead_copy((r + k + 1) % R).start())

    def stat_copy(k):
        to, device = place(k)
        return remote(stats.at[me], stats.at[me], stat_send.at[to], stat_recv.at[me], **device)

    @pl.when(even)
    def _():
        each(R * C - 1, lambda k: stat_copy(k).start())

    def act_edge(src, k):
        return remote(src, act_out.at[0], edge_send.at[k], edge_recv.at[0], section=up)

    def grad_edge(src, k):
        return remote(src, grad_out.at[0], edge_send.at[k], edge_recv.at[1], section=down)

    @pl.when(even)
    def _():
        act_edge(lead.at[r], 0).start()
        h = hid[...].astype(jnp.float32)
        right[...] = (h * gelu_slope(pre[...].astype(jnp.float32))).astype(jnp.bfloat16)

    @pl.when(odd)
    def _():
        grad_edge(lead.at[r], 0).start()
        right[...] = hid[...]

    def part_copy(i, to):
        columns = pl.ds(i * K, K)
        return remote(
            parts.at[to, :, columns], sums.at[r, :, columns],
            part_send.at[i, to], part_recv.at[i, r], row=to,
        )

    for i in range(N):
        weight_copy(i).wait()
        term = lax.dot_general(
            right[...], w[i * K:(i + 1) * K, :], (((1,), (1,)), ((), ())),
            preferred_element_type=jnp.float32,
        )
        for q in range(R):
            parts[q, :, i * K:(i + 1) * K] = term[q * own:(q + 1) * own, :]
        each(R - 1, lambda k: part_copy(i, (r + k + 1) % R).start())

    def lead_arrived(k):
        q = (r + k + 1) % R
        remote(lead.at[q], lead.at[q], lead_send.at[q], lead_recv.at[q], row=q).wait_recv()

    each(R - 1, lead_arrived)

    def stat_arrived(k):
        q, device = place(k)
        remote(stats.at[q], stats.at[q], stat_send.at[q], stat_recv.at[q], **device).wait_recv()

    def factors(q, first):
        total, squares = stats[q * C, first], stats[q * C, first + 1]
        for j in range(1, C):
            total = total + stats[q * C + j, first]
            squares = squares + stats[q * C + j, first + 1]
        average = total / D
        return average, lax.rsqrt(squares / D - average * average + EPSILON)

    @pl.when(even)
    def _():
        each(R * C - 1, stat_arrived)
        for q in range(R):
            rows = slice(q * own, (q + 1) * own)
            average, inverse = factors(q, 0)
            mean[rows, :] = average
            scale[rows, :] = inverse

    for q in range(R):
        x[q * own:(q + 1) * own, :] = lead[q].astype(jnp.float32)

    @pl.when(even)
    def _():
        g, b = gain[pl.ds(layer, 1), :], bias[pl.ds(layer, 1), :]
        m, f = mean[:, :1], scale[:, :1]
        for i in range(N):
            columns = slice(i * K, (i + 1) * K)
            x[:, columns] = (x[:, columns] - m) * f * g[:, columns] + b[:, columns]

    total = jnp.zeros((T, F), jnp.float32)
    for i in range(N):
        columns = slice(i * K, (i + 1) * K)
        total = total + jnp.dot(
            x[:, columns].astype(jnp.bfloat16), w[columns, :], preferred_element_type=jnp.float32
        )
    partial[c] = total

    def col_copy(k):
        to = (c + k + 1) % C
        return remote(partial.at[c], partial.at[c], col_send.at[to], col_recv.at[c], col=to)

    each(C - 1, lambda k: col_copy(k).start())

    def part_arrived(k):
        q = (r + k + 1) % R
        for i in range(N):
            columns = pl.ds(i * K, K)
            remote(
                parts.at[q, :, columns], sums.at[q, :, columns],
                part_send.at[i, q], part_recv.at[i, q], row=q,
            ).wait_recv()

    each(R - 1, part_arrived)
    sums[r] = parts[r]
    term = sums[0]
    for q in range(1, R):
        term = term + sums[q]

    @pl.when(odd)
    def _():
        result[...] = (other[...].astype(jnp.float32) + term).astype(jnp.bfloat16)
        act_edge(result, 1).start()

    def mom_copy(k):
        to = (c + k + 1) % C
        return remote(moments.at[c], moments.at[c], mom_send.at[to], mom_recv.at[c], col=to)

    def saved_hat():
        average, inverse = factors(r, 2)
        return (saved[...].astype(jnp.float32) - average[:, :1]) * inverse[:, :1], inverse[:, :1]

    @pl.when(even)
    def _():
        scaled = term * gain[pl.ds(layer, 1), :]
        sums[0] = scaled
        moments[c, 0] = row_sum(scaled)
        moments[c, 1] = row_sum(scaled * saved_hat()[0])
        each(C - 1, lambda k: mom_copy(k).start())

    def col_arrived(k):
        q = (c + k + 1) % C
        remote(partial.at[q], partial.at[q], col_send.at[q], col_recv.at[q], col=q).wait_recv()

    each(C - 1, col_arrived)
    summed = partial[0]
    for q in range(1, C):
        summed = summed + partial[q]

    @pl.when(even)
    def _():
        hidden[...] = gelu(summed).astype(jnp.bfloat16)

    @pl.when(odd)
    def _():
        hidden[...] = summed.astype(jnp.bfloat16)

    pair = s + 1 - 2 * (s % 2)
    hid_copy = remote(hidden, hid_out.at[0], edge_send.at[2], edge_recv.at[2], section=pair)
    hid_copy.start()

    @pl.when(even)
    def _():
        def mom_arrived(k):
            q = (c + k + 1) % C
            remote(moments.at[q], moments.at[q], mom_send.at[q], mom_recv.at[q], col=q).wait_recv()

        each(C - 1, mom_arrived)
        first, second = moments[0, 0], moments[0, 1]
        for q in range(1, C):
            first = first + moments[q, 0]
            second = second + moments[q, 1]
        first, second = first[:, :1] / D, second[:, :1] / D
        h, inverse = saved_hat()
        moved = other[...].astype(jnp.float32) + inverse * (sums[0] - first - h * second)
        result[...] = moved.astype(jnp.bfloat16)
        grad_edge(result, 1).start()

    act_edge(result, 0).wait_recv()
    grad_edge(result, 0).wait_recv()
    hid_copy.wait()
    for k in range(2):
        act_edge(result, k).wait_send()
    each(R - 1, lambda k: lead_copy((r + k + 1) % R).wait_send())
    for i in range(N):
        each(R - 1, lambda k: part_copy(i, (r + k + 1) % R).wait_send())
    each(C - 1, lambda k: col_copy(k).wait_send())

    @pl.when(even)
    def _():
        each(R * C - 1, lambda k: stat_copy(k).wait_send())
        each(C - 1, lambda k: mom_copy(k).wait_send())


def per_device(S, R, C, *arguments):
    act_in, hid_in, grad_in, saved_in, saved_pre, weights, norm_gain, norm_bias = arguments
    own, DC = act_in.shape[1:]
    T, F = hid_in.shape[1:]
    N = 4
    bf16, f32 = jnp.bfloat16, jnp.float32
    dma = pltpu.SemaphoreType.DMA
    scratch = [
        pltpu.VMEM((DC, F), bf16),
        pltpu.VMEM((R, own, DC), bf16),
        pltpu.VMEM((own, DC), bf16),
        pltpu.VMEM((own, DC), bf16),
        pltpu.VMEM((T, F), bf16),
        pltpu.VMEM((T, F), bf16),
        pltpu.VMEM(norm_gain.shape, f32),
        pltpu.VMEM(norm_bias.shape, f32),
        pltpu.VMEM((T, F), bf16),
        pltpu.VMEM((T, DC), f32),
        pltpu.VMEM((T, LANES), f32),
        pltpu.VMEM((T, LANES), f32),
        pltpu.VMEM((R * C, 4, own, LANES), f32),
        pltpu.VMEM((R, own, DC), f32),
        pltpu.VMEM((R, own, DC), f32),
        pltpu.VMEM((C, T, F), f32),
        pltpu.VMEM((C, 2, own, LANES), f32),
        pltpu.VMEM((T, F), bf16),
        pltpu.VMEM((own, DC), bf16),
        dma((N,)), dma((7,)),
        dma((R,)), dma((R,)),
        dma((R * C,)), dma((R * C,)),
        dma((N, R)), dma((N, R)),
        dma((C,)), dma((C,)),
        dma((C,)), dma((C,)),
        dma((3,)), dma((3,)),
    ]
    flops = 4 * T * F * DC
    moved = 2 * DC * F
    return pl.pallas_call(
        functools.partial(kernel, (S, R, C, own, T, F, DC, N)),
        out_shape=[
            jax.ShapeDtypeStruct(act_in.shape, bf16),
            jax.ShapeDtypeStruct(hid_in.shape, bf16),
            jax.ShapeDtypeStruct(grad_in.shape, bf16),
        ],
        in_specs=[pl.BlockSpec(memory_space=pltpu.HBM)] * 8,
        out_specs=[pl.BlockSpec(memory_space=pl.ANY)] * 3,
        scratch_shapes=scratch,
        compiler_params=pltpu.CompilerParams(
            collective_id=0, has_side_effects=True, vmem_limit_bytes=40 * 2**20
        ),
        cost_estimate=pl.CostEstimate(flops=flops, bytes_accessed=moved, transcendentals=T * F),
    )(*arguments)


def solution(mesh):
    S, R, C = (mesh.shape[name] for name in ("section", "row", "col"))
    in_specs = (
        P("section", "row", "col"),
        P("section", None, "row"),
        P("section", "row", "col"),
        P("section", "row", "col"),
        P("section", None, "row"),
        P("section", "col", "row"),
        P(None, "col"),
        P(None, "col"),
    )
    out_specs = (P("section", "row", "col"), P("section", None, "row"), P("section", "row", "col"))
    return jax.shard_map(
        functools.partial(per_device, S, R, C),
        mesh=mesh, in_specs=in_specs, out_specs=out_specs, check_vma=False,
    )
```

```python
import functools

import jax
import jax.numpy as jnp
from jax import lax
from jax.experimental import pallas as pl
from jax.experimental.pallas import tpu as pltpu
from jax.sharding import PartitionSpec as P

EPSILON = 1e-05
ROOT = 0.7978845608028654
CUBIC = 0.044715
MESH = pl.DeviceIdType.MESH
LANES = 128
LIMIT = 64 * 2**20


def each(count, body):
    if count <= 8:
        for step in range(count):
            body(step)
    else:
        lax.fori_loop(0, count, lambda step, carry: (body(step), carry)[1], 0)


def gelu(x):
    return x * (0.5 * (1.0 + jnp.tanh(ROOT * (x + CUBIC * (x * x * x)))))


def gelu_slope(x):
    t = jnp.tanh(ROOT * (x + CUBIC * (x * x * x)))
    return 0.5 * (1.0 + t) + 0.5 * x * (1.0 - t * t) * (ROOT * (1.0 + 3.0 * CUBIC * (x * x)))


def row_sum(values):
    return jnp.broadcast_to(jnp.sum(values, axis=-1, keepdims=True), (values.shape[0], LANES))


def kernel(
    sizes,
    act_in, hid_in, grad_in, saved_in, pre_in, weights, gain_in, bias_in,
    act_out, hid_out, grad_out,
    w, lead, other, saved, hid, pre, gain, bias, right, x, mean, scale, stats,
    parts, sums, partial, moments, hidden, result,
    w_sem, local_sem, lead_send, lead_recv, stat_send, stat_recv, part_send, part_recv,
    col_send, col_recv, mom_send, mom_recv, edge_send, edge_recv,
):
    S, R, C, own, T, F, DC, N = sizes
    D = DC * C
    K = DC // N
    s, r, c = lax.axis_index("section"), lax.axis_index("row"), lax.axis_index("col")
    even = s % 2 == 0
    odd = s % 2 == 1
    layer = s // 2
    up, down = (s + 1) % S, (s + S - 1) % S
    me = r * C + c

    def local(src, dst, k):
        return pltpu.make_async_copy(src, dst, local_sem.at[k])

    def remote(src, dst, send, recv, **device):
        return pltpu.make_async_remote_copy(
            src_ref=src, dst_ref=dst, send_sem=send, recv_sem=recv,
            device_id=device, device_id_type=MESH,
        )

    @pl.when(even)
    def _():
        local(act_in.at[0], lead.at[r], 0).start()
        local(grad_in.at[0], other, 1).start()

    @pl.when(odd)
    def _():
        local(grad_in.at[0], lead.at[r], 0).start()
        local(act_in.at[0], other, 1).start()

    rest = [(saved_in.at[0], saved, 2), (hid_in.at[0], hid, 3), (pre_in.at[0], pre, 4)]
    rest += [(gain_in, gain, 5), (bias_in, bias, 6)]
    for item in rest:
        local(*item).start()

    def weight_copy(i):
        rows = pl.ds(i * K, K)
        return pltpu.make_async_copy(weights.at[0, rows], w.at[rows], w_sem.at[i])

    for i in range(N):
        weight_copy(i).start()

    barrier = pltpu.get_barrier_semaphore()
    for neighbour in (up, down):
        pl.semaphore_signal(barrier, inc=1, device_id={"section": neighbour}, device_id_type=MESH)

    def place(k):
        to = (me + k + 1) % (R * C)
        return to, {"row": to // C, "col": to % C}

    def greet(k):
        pl.semaphore_signal(barrier, inc=1, device_id=place(k)[1], device_id_type=MESH)

    each(R * C - 1, greet)

    local(act_in.at[0], lead.at[r], 0).wait()
    local(act_in.at[0], other, 1).wait()
    for item in rest:
        local(*item).wait()

    @pl.when(even)
    def _():
        v = lead[r].astype(jnp.float32)
        z = saved[...].astype(jnp.float32)
        stats[me, 0] = row_sum(v)
        stats[me, 1] = row_sum(v * v)
        stats[me, 2] = row_sum(z)
        stats[me, 3] = row_sum(z * z)

    pl.semaphore_wait(barrier, R * C + 1)

    def lead_copy(to):
        return remote(lead.at[r], lead.at[r], lead_send.at[to], lead_recv.at[r], row=to)

    each(R - 1, lambda k: lead_copy((r + k + 1) % R).start())

    def stat_copy(k):
        to, device = place(k)
        return remote(stats.at[me], stats.at[me], stat_send.at[to], stat_recv.at[me], **device)

    @pl.when(even)
    def _():
        each(R * C - 1, lambda k: stat_copy(k).start())

    def act_edge(src, k):
        return remote(src, act_out.at[0], edge_send.at[k], edge_recv.at[0], section=up)

    def grad_edge(src, k):
        return remote(src, grad_out.at[0], edge_send.at[k], edge_recv.at[1], section=down)

    @pl.when(even)
    def _():
        act_edge(lead.at[r], 0).start()
        h = hid[...].astype(jnp.float32)
        right[...] = (h * gelu_slope(pre[...].astype(jnp.float32))).astype(jnp.bfloat16)

    @pl.when(odd)
    def _():
        grad_edge(lead.at[r], 0).start()
        right[...] = hid[...]

    def part_copy(i, to):
        columns = pl.ds(i * K, K)
        return remote(
            parts.at[to, :, columns], sums.at[r, :, columns],
            part_send.at[i, to], part_recv.at[i, r], row=to,
        )

    for i in range(N):
        weight_copy(i).wait()
        term = lax.dot_general(
            right[...], w[i * K:(i + 1) * K, :], (((1,), (1,)), ((), ())),
            preferred_element_type=jnp.float32,
        )
        for q in range(R):
            parts[q, :, i * K:(i + 1) * K] = term[q * own:(q + 1) * own, :]
        each(R - 1, lambda k: part_copy(i, (r + k + 1) % R).start())

    def lead_arrived(k):
        q = (r + k + 1) % R
        remote(lead.at[q], lead.at[q], lead_send.at[q], lead_recv.at[q], row=q).wait_recv()

    each(R - 1, lead_arrived)

    def stat_arrived(k):
        q, device = place(k)
        remote(stats.at[q], stats.at[q], stat_send.at[q], stat_recv.at[q], **device).wait_recv()

    def factors(q, first):
        total, squares = stats[q * C, first], stats[q * C, first + 1]
        for j in range(1, C):
            total = total + stats[q * C + j, first]
            squares = squares + stats[q * C + j, first + 1]
        average = total / D
        return average, lax.rsqrt(squares / D - average * average + EPSILON)

    @pl.when(even)
    def _():
        each(R * C - 1, stat_arrived)
        for q in range(R):
            rows = slice(q * own, (q + 1) * own)
            average, inverse = factors(q, 0)
            mean[rows, :] = average
            scale[rows, :] = inverse

    for q in range(R):
        x[q * own:(q + 1) * own, :] = lead[q].astype(jnp.float32)

    @pl.when(even)
    def _():
        g, b = gain[pl.ds(layer, 1), :], bias[pl.ds(layer, 1), :]
        m, f = mean[:, :1], scale[:, :1]
        for i in range(N):
            columns = slice(i * K, (i + 1) * K)
            x[:, columns] = (x[:, columns] - m) * f * g[:, columns] + b[:, columns]

    total = jnp.zeros((T, F), jnp.float32)
    for i in range(N):
        columns = slice(i * K, (i + 1) * K)
        total = total + jnp.dot(
            x[:, columns].astype(jnp.bfloat16), w[columns, :], preferred_element_type=jnp.float32
        )
    partial[c] = total

    def col_copy(k):
        to = (c + k + 1) % C
        return remote(partial.at[c], partial.at[c], col_send.at[to], col_recv.at[c], col=to)

    each(C - 1, lambda k: col_copy(k).start())

    def part_arrived(k):
        q = (r + k + 1) % R
        for i in range(N):
            columns = pl.ds(i * K, K)
            remote(
                parts.at[q, :, columns], sums.at[q, :, columns],
                part_send.at[i, q], part_recv.at[i, q], row=q,
            ).wait_recv()

    each(R - 1, part_arrived)
    sums[r] = parts[r]
    term = sums[0]
    for q in range(1, R):
        term = term + sums[q]

    @pl.when(odd)
    def _():
        result[...] = (other[...].astype(jnp.float32) + term).astype(jnp.bfloat16)
        act_edge(result, 1).start()

    def mom_copy(k):
        to = (c + k + 1) % C
        return remote(moments.at[c], moments.at[c], mom_send.at[to], mom_recv.at[c], col=to)

    def saved_hat():
        average, inverse = factors(r, 2)
        return (saved[...].astype(jnp.float32) - average[:, :1]) * inverse[:, :1], inverse[:, :1]

    @pl.when(even)
    def _():
        scaled = term * gain[pl.ds(layer, 1), :]
        sums[0] = scaled
        moments[c, 0] = row_sum(scaled)
        moments[c, 1] = row_sum(scaled * saved_hat()[0])
        each(C - 1, lambda k: mom_copy(k).start())

    def col_arrived(k):
        q = (c + k + 1) % C
        remote(partial.at[q], partial.at[q], col_send.at[q], col_recv.at[q], col=q).wait_recv()

    each(C - 1, col_arrived)
    summed = partial[0]
    for q in range(1, C):
        summed = summed + partial[q]

    @pl.when(even)
    def _():
        hidden[...] = gelu(summed).astype(jnp.bfloat16)

    @pl.when(odd)
    def _():
        hidden[...] = summed.astype(jnp.bfloat16)

    pair = s + 1 - 2 * (s % 2)
    hid_copy = remote(hidden, hid_out.at[0], edge_send.at[2], edge_recv.at[2], section=pair)
    hid_copy.start()

    @pl.when(even)
    def _():
        def mom_arrived(k):
            q = (c + k + 1) % C
            remote(moments.at[q], moments.at[q], mom_send.at[q], mom_recv.at[q], col=q).wait_recv()

        each(C - 1, mom_arrived)
        first, second = moments[0, 0], moments[0, 1]
        for q in range(1, C):
            first = first + moments[q, 0]
            second = second + moments[q, 1]
        first, second = first[:, :1] / D, second[:, :1] / D
        h, inverse = saved_hat()
        moved = other[...].astype(jnp.float32) + inverse * (sums[0] - first - h * second)
        result[...] = moved.astype(jnp.bfloat16)
        grad_edge(result, 1).start()

    act_edge(result, 0).wait_recv()
    grad_edge(result, 0).wait_recv()
    hid_copy.wait()
    for k in range(2):
        act_edge(result, k).wait_send()
    each(R - 1, lambda k: lead_copy((r + k + 1) % R).wait_send())
    for i in range(N):
        each(R - 1, lambda k: part_copy(i, (r + k + 1) % R).wait_send())
    each(C - 1, lambda k: col_copy(k).wait_send())

    @pl.when(even)
    def _():
        each(R * C - 1, lambda k: stat_copy(k).wait_send())
        each(C - 1, lambda k: mom_copy(k).wait_send())


def write_out(a, b, c, a_out, b_out, c_out, sem):
    pairs = ((a, a_out), (b, b_out), (c, c_out))
    copies = [pltpu.make_async_copy(i, o, sem.at[k]) for k, (i, o) in enumerate(pairs)]
    for copy in copies:
        copy.start()
    for copy in copies:
        copy.wait()


def per_device(S, R, C, *arguments):
    act_in, hid_in, grad_in, saved_in, saved_pre, weights, norm_gain, norm_bias = arguments
    own, DC = act_in.shape[1:]
    T, F = hid_in.shape[1:]
    N = 4
    bf16, f32 = jnp.bfloat16, jnp.float32
    dma = pltpu.SemaphoreType.DMA
    scratch = [
        pltpu.VMEM((DC, F), bf16),
        pltpu.VMEM((R, own, DC), bf16),
        pltpu.VMEM((own, DC), bf16),
        pltpu.VMEM((own, DC), bf16),
        pltpu.VMEM((T, F), bf16),
        pltpu.VMEM((T, F), bf16),
        pltpu.VMEM(norm_gain.shape, f32),
        pltpu.VMEM(norm_bias.shape, f32),
        pltpu.VMEM((T, F), bf16),
        pltpu.VMEM((T, DC), f32),
        pltpu.VMEM((T, LANES), f32),
        pltpu.VMEM((T, LANES), f32),
        pltpu.VMEM((R * C, 4, own, LANES), f32),
        pltpu.VMEM((R, own, DC), f32),
        pltpu.VMEM((R, own, DC), f32),
        pltpu.VMEM((C, T, F), f32),
        pltpu.VMEM((C, 2, own, LANES), f32),
        pltpu.VMEM((T, F), bf16),
        pltpu.VMEM((own, DC), bf16),
        dma((N,)), dma((7,)),
        dma((R,)), dma((R,)),
        dma((R * C,)), dma((R * C,)),
        dma((N, R)), dma((N, R)),
        dma((C,)), dma((C,)),
        dma((C,)), dma((C,)),
        dma((3,)), dma((3,)),
    ]
    flops = 4 * T * F * DC
    moved = 2 * DC * F
    results = pl.pallas_call(
        functools.partial(kernel, (S, R, C, own, T, F, DC, N)),
        out_shape=[
            jax.ShapeDtypeStruct(act_in.shape, bf16),
            jax.ShapeDtypeStruct(hid_in.shape, bf16),
            jax.ShapeDtypeStruct(grad_in.shape, bf16),
        ],
        in_specs=[pl.BlockSpec(memory_space=pltpu.HBM)] * 8,
        out_specs=[pl.BlockSpec(memory_space=pl.ANY)] * 3,
        scratch_shapes=scratch,
        compiler_params=pltpu.CompilerParams(
            collective_id=0, has_side_effects=True, vmem_limit_bytes=LIMIT
        ),
        cost_estimate=pl.CostEstimate(flops=flops, bytes_accessed=moved, transcendentals=T * F),
    )(*arguments)
    return pl.pallas_call(
        write_out,
        out_shape=[jax.ShapeDtypeStruct(a.shape, a.dtype) for a in results],
        in_specs=[pl.BlockSpec(memory_space=pl.ANY)] * 3,
        out_specs=[pl.BlockSpec(memory_space=pl.ANY)] * 3,
        scratch_shapes=[dma((3,))],
        compiler_params=pltpu.CompilerParams(vmem_limit_bytes=LIMIT),
    )(*results)


def solution(mesh):
    S, R, C = (mesh.shape[name] for name in ("section", "row", "col"))
    in_specs = (
        P("section", "row", "col"),
        P("section", None, "row"),
        P("section", "row", "col"),
        P("section", "row", "col"),
        P("section", None, "row"),
        P("section", "col", "row"),
        P(None, "col"),
        P(None, "col"),
    )
    out_specs = (P("section", "row", "col"), P("section", None, "row"), P("section", "row", "col"))
    return jax.shard_map(
        functools.partial(per_device, S, R, C),
        mesh=mesh, in_specs=in_specs, out_specs=out_specs, check_vma=False,
    )
```

```python
import functools

import jax
import jax.numpy as jnp
from jax import lax
from jax.experimental import pallas as pl
from jax.experimental.pallas import tpu as pltpu
from jax.sharding import PartitionSpec as P

EPSILON = 1e-05
ROOT = 0.7978845608028654
CUBIC = 0.044715
MESH = pl.DeviceIdType.MESH
LANES = 128
LIMIT = 48 * 2**20


def each(count, body):
    if count <= 8:
        for step in range(count):
            body(step)
    else:
        lax.fori_loop(0, count, lambda step, carry: (body(step), carry)[1], 0)


def gelu(x):
    return x * (0.5 * (1.0 + jnp.tanh(ROOT * (x + CUBIC * (x * x * x)))))


def gelu_slope(x):
    t = jnp.tanh(ROOT * (x + CUBIC * (x * x * x)))
    return 0.5 * (1.0 + t) + 0.5 * x * (1.0 - t * t) * (ROOT * (1.0 + 3.0 * CUBIC * (x * x)))


def row_sum(values):
    return jnp.broadcast_to(jnp.sum(values, axis=-1, keepdims=True), (values.shape[0], LANES))


def kernel(
    sizes,
    act_in, hid_in, grad_in, saved_in, pre_in, weights, gain_in, bias_in,
    act_out, hid_out, grad_out,
    w, lead, other, saved, hid, pre, gain, bias, right, x, mean, scale, stats,
    parts, sums, partial, moments, hidden, result,
    w_sem, local_sem, lead_send, lead_recv, stat_send, stat_recv, part_send, part_recv,
    col_send, col_recv, mom_send, mom_recv, edge_send, edge_recv,
):
    S, R, C, own, T, F, DC, N = sizes
    D = DC * C
    K = DC // N
    s, r, c = lax.axis_index("section"), lax.axis_index("row"), lax.axis_index("col")
    even = s % 2 == 0
    odd = s % 2 == 1
    layer = s // 2
    up, down = (s + 1) % S, (s + S - 1) % S
    me = r * C + c

    def local(src, dst, k):
        return pltpu.make_async_copy(src, dst, local_sem.at[k])

    def remote(src, dst, send, recv, **device):
        return pltpu.make_async_remote_copy(
            src_ref=src, dst_ref=dst, send_sem=send, recv_sem=recv,
            device_id=device, device_id_type=MESH,
        )

    @pl.when(even)
    def _():
        local(act_in.at[0], lead.at[r], 0).start()
        local(grad_in.at[0], other, 1).start()

    @pl.when(odd)
    def _():
        local(grad_in.at[0], lead.at[r], 0).start()
        local(act_in.at[0], other, 1).start()

    rest = [(saved_in.at[0], saved, 2), (hid_in.at[0], hid, 3), (pre_in.at[0], pre, 4)]
    rest += [(gain_in, gain, 5), (bias_in, bias, 6)]
    for item in rest:
        local(*item).start()

    def weight_copy(i):
        rows = pl.ds(i * K, K)
        return pltpu.make_async_copy(weights.at[0, rows], w.at[rows], w_sem.at[i])

    for i in range(N):
        weight_copy(i).start()

    barrier = pltpu.get_barrier_semaphore()
    for neighbour in (up, down):
        pl.semaphore_signal(barrier, inc=1, device_id={"section": neighbour}, device_id_type=MESH)

    def place(k):
        to = (me + k + 1) % (R * C)
        return to, {"row": to // C, "col": to % C}

    def greet(k):
        pl.semaphore_signal(barrier, inc=1, device_id=place(k)[1], device_id_type=MESH)

    each(R * C - 1, greet)

    local(act_in.at[0], lead.at[r], 0).wait()
    local(act_in.at[0], other, 1).wait()
    for item in rest:
        local(*item).wait()

    @pl.when(even)
    def _():
        v = lead[r].astype(jnp.float32)
        z = saved[...].astype(jnp.float32)
        stats[me, 0] = row_sum(v)
        stats[me, 1] = row_sum(v * v)
        stats[me, 2] = row_sum(z)
        stats[me, 3] = row_sum(z * z)

    pl.semaphore_wait(barrier, R * C + 1)

    def lead_copy(to):
        return remote(lead.at[r], lead.at[r], lead_send.at[to], lead_recv.at[r], row=to)

    each(R - 1, lambda k: lead_copy((r + k + 1) % R).start())

    def stat_copy(k):
        to, device = place(k)
        return remote(stats.at[me], stats.at[me], stat_send.at[to], stat_recv.at[me], **device)

    @pl.when(even)
    def _():
        each(R * C - 1, lambda k: stat_copy(k).start())

    def act_edge(src, k):
        return remote(src, act_out.at[0], edge_send.at[k], edge_recv.at[0], section=up)

    def grad_edge(src, k):
        return remote(src, grad_out.at[0], edge_send.at[k], edge_recv.at[1], section=down)

    @pl.when(even)
    def _():
        act_edge(lead.at[r], 0).start()
        h = hid[...].astype(jnp.float32)
        right[...] = (h * gelu_slope(pre[...].astype(jnp.float32))).astype(jnp.bfloat16)

    @pl.when(odd)
    def _():
        grad_edge(lead.at[r], 0).start()
        right[...] = hid[...]

    def part_copy(i, to):
        columns = pl.ds(i * K, K)
        return remote(
            parts.at[to, :, columns], sums.at[r, :, columns],
            part_send.at[i, to], part_recv.at[i, r], row=to,
        )

    for i in range(N):
        weight_copy(i).wait()
        term = lax.dot_general(
            right[...], w[i * K:(i + 1) * K, :], (((1,), (1,)), ((), ())),
            preferred_element_type=jnp.float32,
        )
        for q in range(R):
            parts[q, :, i * K:(i + 1) * K] = term[q * own:(q + 1) * own, :]
        each(R - 1, lambda k: part_copy(i, (r + k + 1) % R).start())

    def lead_arrived(k):
        q = (r + k + 1) % R
        remote(lead.at[q], lead.at[q], lead_send.at[q], lead_recv.at[q], row=q).wait_recv()

    each(R - 1, lead_arrived)

    def stat_arrived(k):
        q, device = place(k)
        remote(stats.at[q], stats.at[q], stat_send.at[q], stat_recv.at[q], **device).wait_recv()

    def factors(q, first):
        total, squares = stats[q * C, first], stats[q * C, first + 1]
        for j in range(1, C):
            total = total + stats[q * C + j, first]
            squares = squares + stats[q * C + j, first + 1]
        average = total / D
        return average, lax.rsqrt(squares / D - average * average + EPSILON)

    @pl.when(even)
    def _():
        each(R * C - 1, stat_arrived)
        for q in range(R):
            rows = slice(q * own, (q + 1) * own)
            average, inverse = factors(q, 0)
            mean[rows, :] = average
            scale[rows, :] = inverse

    for q in range(R):
        x[q * own:(q + 1) * own, :] = lead[q].astype(jnp.float32)

    @pl.when(even)
    def _():
        g, b = gain[pl.ds(layer, 1), :], bias[pl.ds(layer, 1), :]
        m, f = mean[:, :1], scale[:, :1]
        for i in range(N):
            columns = slice(i * K, (i + 1) * K)
            x[:, columns] = (x[:, columns] - m) * f * g[:, columns] + b[:, columns]

    total = jnp.zeros((T, F), jnp.float32)
    for i in range(N):
        columns = slice(i * K, (i + 1) * K)
        total = total + jnp.dot(
            x[:, columns].astype(jnp.bfloat16), w[columns, :], preferred_element_type=jnp.float32
        )
    partial[c] = total

    def col_copy(k):
        to = (c + k + 1) % C
        return remote(partial.at[c], partial.at[c], col_send.at[to], col_recv.at[c], col=to)

    each(C - 1, lambda k: col_copy(k).start())

    def part_arrived(k):
        q = (r + k + 1) % R
        for i in range(N):
            columns = pl.ds(i * K, K)
            remote(
                parts.at[q, :, columns], sums.at[q, :, columns],
                part_send.at[i, q], part_recv.at[i, q], row=q,
            ).wait_recv()

    each(R - 1, part_arrived)
    sums[r] = parts[r]
    term = sums[0]
    for q in range(1, R):
        term = term + sums[q]

    @pl.when(odd)
    def _():
        result[...] = (other[...].astype(jnp.float32) + term).astype(jnp.bfloat16)
        act_edge(result, 1).start()

    def mom_copy(k):
        to = (c + k + 1) % C
        return remote(moments.at[c], moments.at[c], mom_send.at[to], mom_recv.at[c], col=to)

    def saved_hat():
        average, inverse = factors(r, 2)
        return (saved[...].astype(jnp.float32) - average[:, :1]) * inverse[:, :1], inverse[:, :1]

    @pl.when(even)
    def _():
        scaled = term * gain[pl.ds(layer, 1), :]
        sums[0] = scaled
        moments[c, 0] = row_sum(scaled)
        moments[c, 1] = row_sum(scaled * saved_hat()[0])
        each(C - 1, lambda k: mom_copy(k).start())

    def col_arrived(k):
        q = (c + k + 1) % C
        remote(partial.at[q], partial.at[q], col_send.at[q], col_recv.at[q], col=q).wait_recv()

    each(C - 1, col_arrived)
    summed = partial[0]
    for q in range(1, C):
        summed = summed + partial[q]

    @pl.when(even)
    def _():
        hidden[...] = gelu(summed).astype(jnp.bfloat16)

    @pl.when(odd)
    def _():
        hidden[...] = summed.astype(jnp.bfloat16)

    pair = s + 1 - 2 * (s % 2)
    hid_copy = remote(hidden, hid_out.at[0], edge_send.at[2], edge_recv.at[2], section=pair)
    hid_copy.start()

    @pl.when(even)
    def _():
        def mom_arrived(k):
            q = (c + k + 1) % C
            remote(moments.at[q], moments.at[q], mom_send.at[q], mom_recv.at[q], col=q).wait_recv()

        each(C - 1, mom_arrived)
        first, second = moments[0, 0], moments[0, 1]
        for q in range(1, C):
            first = first + moments[q, 0]
            second = second + moments[q, 1]
        first, second = first[:, :1] / D, second[:, :1] / D
        h, inverse = saved_hat()
        moved = other[...].astype(jnp.float32) + inverse * (sums[0] - first - h * second)
        result[...] = moved.astype(jnp.bfloat16)
        grad_edge(result, 1).start()

    act_edge(result, 0).wait_recv()
    grad_edge(result, 0).wait_recv()
    hid_copy.wait()
    for k in range(2):
        act_edge(result, k).wait_send()
    each(R - 1, lambda k: lead_copy((r + k + 1) % R).wait_send())
    for i in range(N):
        each(R - 1, lambda k: part_copy(i, (r + k + 1) % R).wait_send())
    each(C - 1, lambda k: col_copy(k).wait_send())

    @pl.when(even)
    def _():
        each(R * C - 1, lambda k: stat_copy(k).wait_send())
        each(C - 1, lambda k: mom_copy(k).wait_send())


def write_out(a, b, c, a_out, b_out, c_out, sem):
    pairs = ((a, a_out), (b, b_out), (c, c_out))
    copies = [pltpu.make_async_copy(i, o, sem.at[k]) for k, (i, o) in enumerate(pairs)]
    for copy in copies:
        copy.start()
    for copy in copies:
        copy.wait()


def per_device(S, R, C, *arguments):
    act_in, hid_in, grad_in, saved_in, saved_pre, weights, norm_gain, norm_bias = arguments
    own, DC = act_in.shape[1:]
    T, F = hid_in.shape[1:]
    N = 4
    bf16, f32 = jnp.bfloat16, jnp.float32
    dma = pltpu.SemaphoreType.DMA
    scratch = [
        pltpu.VMEM((DC, F), bf16),
        pltpu.VMEM((R, own, DC), bf16),
        pltpu.VMEM((own, DC), bf16),
        pltpu.VMEM((own, DC), bf16),
        pltpu.VMEM((T, F), bf16),
        pltpu.VMEM((T, F), bf16),
        pltpu.VMEM(norm_gain.shape, f32),
        pltpu.VMEM(norm_bias.shape, f32),
        pltpu.VMEM((T, F), bf16),
        pltpu.VMEM((T, DC), f32),
        pltpu.VMEM((T, LANES), f32),
        pltpu.VMEM((T, LANES), f32),
        pltpu.VMEM((R * C, 4, own, LANES), f32),
        pltpu.VMEM((R, own, DC), f32),
        pltpu.VMEM((R, own, DC), f32),
        pltpu.VMEM((C, T, F), f32),
        pltpu.VMEM((C, 2, own, LANES), f32),
        pltpu.VMEM((T, F), bf16),
        pltpu.VMEM((own, DC), bf16),
        dma((N,)), dma((7,)),
        dma((R,)), dma((R,)),
        dma((R * C,)), dma((R * C,)),
        dma((N, R)), dma((N, R)),
        dma((C,)), dma((C,)),
        dma((C,)), dma((C,)),
        dma((3,)), dma((3,)),
    ]
    flops = 4 * T * F * DC
    moved = 2 * DC * F
    results = pl.pallas_call(
        functools.partial(kernel, (S, R, C, own, T, F, DC, N)),
        out_shape=[
            pltpu.VMEM(act_in.shape, bf16),
            pltpu.VMEM(hid_in.shape, bf16),
            pltpu.VMEM(grad_in.shape, bf16),
        ],
        in_specs=[pl.BlockSpec(memory_space=pl.ANY)] * 8,
        out_specs=[pl.BlockSpec(memory_space=pl.ANY)] * 3,
        scratch_shapes=scratch,
        compiler_params=pltpu.CompilerParams(
            collective_id=0, has_side_effects=True, vmem_limit_bytes=LIMIT
        ),
        cost_estimate=pl.CostEstimate(flops=flops, bytes_accessed=moved, transcendentals=T * F),
    )(*(pltpu.with_memory_space_constraint(a, pltpu.HBM) for a in arguments))
    return pl.pallas_call(
        write_out,
        out_shape=[jax.ShapeDtypeStruct(a.shape, a.dtype) for a in results],
        in_specs=[pl.BlockSpec(memory_space=pl.ANY)] * 3,
        out_specs=[pl.BlockSpec(memory_space=pl.ANY)] * 3,
        scratch_shapes=[dma((3,))],
        compiler_params=pltpu.CompilerParams(vmem_limit_bytes=LIMIT),
    )(*results)


def solution(mesh):
    S, R, C = (mesh.shape[name] for name in ("section", "row", "col"))
    in_specs = (
        P("section", "row", "col"),
        P("section", None, "row"),
        P("section", "row", "col"),
        P("section", "row", "col"),
        P("section", None, "row"),
        P("section", "col", "row"),
        P(None, "col"),
        P(None, "col"),
    )
    out_specs = (P("section", "row", "col"), P("section", None, "row"), P("section", "row", "col"))
    return jax.shard_map(
        functools.partial(per_device, S, R, C),
        mesh=mesh, in_specs=in_specs, out_specs=out_specs, check_vma=False,
    )
```

```python
import functools

import jax
import jax.numpy as jnp
from jax import lax
from jax.experimental import pallas as pl
from jax.experimental.pallas import tpu as pltpu
from jax.sharding import PartitionSpec as P

EPSILON = 1e-05
ROOT = 0.7978845608028654
CUBIC = 0.044715
MESH = pl.DeviceIdType.MESH
LANES = 128
LIMIT = 48 * 2**20


def each(count, body):
    if count <= 8:
        for step in range(count):
            body(step)
    else:
        lax.fori_loop(0, count, lambda step, carry: (body(step), carry)[1], 0)


def gelu(x):
    return x * (0.5 * (1.0 + jnp.tanh(ROOT * (x + CUBIC * (x * x * x)))))


def gelu_slope(x):
    t = jnp.tanh(ROOT * (x + CUBIC * (x * x * x)))
    return 0.5 * (1.0 + t) + 0.5 * x * (1.0 - t * t) * (ROOT * (1.0 + 3.0 * CUBIC * (x * x)))


def row_sum(values):
    return jnp.broadcast_to(jnp.sum(values, axis=-1, keepdims=True), (values.shape[0], LANES))


def kernel(
    sizes,
    act_in, hid_in, grad_in, saved_in, pre_in, weights, gain_in, bias_in,
    act_out, hid_out, grad_out,
    w, lead, other, saved, hid, pre, gain, bias, right, x, mean, scale, stats,
    parts, sums, partial, moments, hidden, result,
    w_sem, local_sem, lead_send, lead_recv, stat_send, stat_recv, part_send, part_recv,
    col_send, col_recv, mom_send, mom_recv, edge_send, edge_recv,
):
    S, R, C, own, T, F, DC, N = sizes
    D = DC * C
    K = DC // N
    s, r, c = lax.axis_index("section"), lax.axis_index("row"), lax.axis_index("col")
    even = s % 2 == 0
    odd = s % 2 == 1
    layer = s // 2
    up, down = (s + 1) % S, (s + S - 1) % S
    me = r * C + c

    def local(src, dst, k):
        return pltpu.make_async_copy(src, dst, local_sem.at[k])

    def remote(src, dst, send, recv, **device):
        return pltpu.make_async_remote_copy(
            src_ref=src, dst_ref=dst, send_sem=send, recv_sem=recv,
            device_id=device, device_id_type=MESH,
        )

    barrier = pltpu.get_barrier_semaphore()
    for neighbour in (up, down):
        pl.semaphore_signal(barrier, inc=1, device_id={"section": neighbour}, device_id_type=MESH)

    def place(k):
        to = (me + k + 1) % (R * C)
        return to, {"row": to // C, "col": to % C}

    def greet(k):
        pl.semaphore_signal(barrier, inc=1, device_id=place(k)[1], device_id_type=MESH)

    each(R * C - 1, greet)

    @pl.when(even)
    def _():
        local(act_in.at[0], lead.at[r], 0).start()
        local(grad_in.at[0], other, 1).start()

    @pl.when(odd)
    def _():
        local(grad_in.at[0], lead.at[r], 0).start()
        local(act_in.at[0], other, 1).start()

    local_saved = local(saved_in.at[0], saved, 2)
    local_hid, local_pre = local(hid_in.at[0], hid, 3), local(pre_in.at[0], pre, 4)
    local_gain, local_bias = local(gain_in, gain, 5), local(bias_in, bias, 6)
    for copy in (local_saved, local_hid, local_pre):
        copy.start()

    def weight_copy(i):
        rows = pl.ds(i * K, K)
        return pltpu.make_async_copy(weights.at[0, rows], w.at[rows], w_sem.at[i])

    for i in range(N):
        weight_copy(i).start()
    local_gain.start()
    local_bias.start()

    pl.semaphore_wait(barrier, R * C + 1)

    def lead_copy(src, to):
        return remote(src, lead.at[r], lead_send.at[to], lead_recv.at[r], row=to)

    @pl.when(even)
    def _():
        each(R - 1, lambda k: lead_copy(act_in.at[0], (r + k + 1) % R).start())

    @pl.when(odd)
    def _():
        each(R - 1, lambda k: lead_copy(grad_in.at[0], (r + k + 1) % R).start())

    def stat_copy(k):
        to, device = place(k)
        return remote(stats.at[me], stats.at[me], stat_send.at[to], stat_recv.at[me], **device)

    local(act_in.at[0], lead.at[r], 0).wait()
    local_saved.wait()

    @pl.when(even)
    def _():
        v = lead[r].astype(jnp.float32)
        z = saved[...].astype(jnp.float32)
        stats[me, 0] = row_sum(v)
        stats[me, 1] = row_sum(v * v)
        stats[me, 2] = row_sum(z)
        stats[me, 3] = row_sum(z * z)
        each(R * C - 1, lambda k: stat_copy(k).start())

    local_hid.wait()
    local_pre.wait()

    def act_edge(src, k):
        return remote(src, act_out.at[0], edge_send.at[k], edge_recv.at[0], section=up)

    def grad_edge(src, k):
        return remote(src, grad_out.at[0], edge_send.at[k], edge_recv.at[1], section=down)

    @pl.when(even)
    def _():
        act_edge(lead.at[r], 0).start()
        h = hid[...].astype(jnp.float32)
        right[...] = (h * gelu_slope(pre[...].astype(jnp.float32))).astype(jnp.bfloat16)

    @pl.when(odd)
    def _():
        grad_edge(lead.at[r], 0).start()
        right[...] = hid[...]

    G = N // 2
    wide = DC // G

    def part_copy(i, to):
        columns = pl.ds(i * wide, wide)
        return remote(
            parts.at[to, :, columns], sums.at[r, :, columns],
            part_send.at[i, to], part_recv.at[i, r], row=to,
        )

    for i in range(N):
        weight_copy(i).wait()
        term = lax.dot_general(
            right[...], w[i * K:(i + 1) * K, :], (((1,), (1,)), ((), ())),
            preferred_element_type=jnp.float32,
        )
        for q in range(R):
            parts[q, :, i * K:(i + 1) * K] = term[q * own:(q + 1) * own, :]
        if i % 2 == 1:
            each(R - 1, lambda k: part_copy(i // 2, (r + k + 1) % R).start())

    def lead_arrived(k):
        q = (r + k + 1) % R
        remote(lead.at[q], lead.at[q], lead_send.at[q], lead_recv.at[q], row=q).wait_recv()

    each(R - 1, lead_arrived)

    def stat_arrived(k):
        q, device = place(k)
        remote(stats.at[q], stats.at[q], stat_send.at[q], stat_recv.at[q], **device).wait_recv()

    def factors(q, first):
        total, squares = stats[q * C, first], stats[q * C, first + 1]
        for j in range(1, C):
            total = total + stats[q * C + j, first]
            squares = squares + stats[q * C + j, first + 1]
        average = total / D
        return average, lax.rsqrt(squares / D - average * average + EPSILON)

    @pl.when(even)
    def _():
        each(R * C - 1, stat_arrived)
        for q in range(R):
            rows = slice(q * own, (q + 1) * own)
            average, inverse = factors(q, 0)
            mean[rows, :] = average
            scale[rows, :] = inverse

    for q in range(R):
        x[q * own:(q + 1) * own, :] = lead[q].astype(jnp.float32)

    local(act_in.at[0], other, 1).wait()
    local_gain.wait()
    local_bias.wait()

    def half(first):
        spans = range(first, first + N // 2)

        def product(left):
            total = jnp.zeros((T, F), jnp.float32)
            for i in spans:
                columns = slice(i * K, (i + 1) * K)
                total = total + jnp.dot(
                    left(columns).astype(jnp.bfloat16), w[columns, :],
                    preferred_element_type=jnp.float32,
                )
            return total

        def keep(total):
            partial[c] = total if first == 0 else partial[c] + total

        @pl.when(even)
        def _():
            m, f = mean[:, :1], scale[:, :1]

            def normed(columns):
                g, b = gain[pl.ds(layer, 1), columns], bias[pl.ds(layer, 1), columns]
                return (x[:, columns] - m) * f * g + b

            keep(product(normed))

        @pl.when(odd)
        def _():
            keep(product(lambda columns: x[:, columns]))

    half(0)

    def col_copy(k):
        to = (c + k + 1) % C
        return remote(partial.at[c], partial.at[c], col_send.at[to], col_recv.at[c], col=to)

    def part_arrived(k):
        q = (r + k + 1) % R
        for i in range(G):
            columns = pl.ds(i * wide, wide)
            remote(
                parts.at[q, :, columns], sums.at[q, :, columns],
                part_send.at[i, q], part_recv.at[i, q], row=q,
            ).wait_recv()

    each(R - 1, part_arrived)
    sums[r] = parts[r]
    term = sums[0]
    for q in range(1, R):
        term = term + sums[q]

    @pl.when(odd)
    def _():
        result[...] = (other[...].astype(jnp.float32) + term).astype(jnp.bfloat16)
        act_edge(result, 1).start()

    def mom_copy(k):
        to = (c + k + 1) % C
        return remote(moments.at[c], moments.at[c], mom_send.at[to], mom_recv.at[c], col=to)

    def saved_hat():
        average, inverse = factors(r, 2)
        return (saved[...].astype(jnp.float32) - average[:, :1]) * inverse[:, :1], inverse[:, :1]

    @pl.when(even)
    def _():
        scaled = term * gain[pl.ds(layer, 1), :]
        sums[0] = scaled
        moments[c, 0] = row_sum(scaled)
        moments[c, 1] = row_sum(scaled * saved_hat()[0])
        each(C - 1, lambda k: mom_copy(k).start())

    half(N // 2)
    each(C - 1, lambda k: col_copy(k).start())

    @pl.when(even)
    def _():
        def mom_arrived(k):
            q = (c + k + 1) % C
            remote(moments.at[q], moments.at[q], mom_send.at[q], mom_recv.at[q], col=q).wait_recv()

        each(C - 1, mom_arrived)
        first, second = moments[0, 0], moments[0, 1]
        for q in range(1, C):
            first = first + moments[q, 0]
            second = second + moments[q, 1]
        first, second = first[:, :1] / D, second[:, :1] / D
        h, inverse = saved_hat()
        moved = other[...].astype(jnp.float32) + inverse * (sums[0] - first - h * second)
        result[...] = moved.astype(jnp.bfloat16)
        grad_edge(result, 1).start()

    def col_arrived(k):
        q = (c + k + 1) % C
        remote(partial.at[q], partial.at[q], col_send.at[q], col_recv.at[q], col=q).wait_recv()

    each(C - 1, col_arrived)
    summed = partial[0]
    for q in range(1, C):
        summed = summed + partial[q]

    @pl.when(even)
    def _():
        hidden[...] = gelu(summed).astype(jnp.bfloat16)

    @pl.when(odd)
    def _():
        hidden[...] = summed.astype(jnp.bfloat16)

    pair = s + 1 - 2 * (s % 2)
    hid_copy = remote(hidden, hid_out.at[0], edge_send.at[2], edge_recv.at[2], section=pair)
    hid_copy.start()

    act_edge(result, 0).wait_recv()
    grad_edge(result, 0).wait_recv()
    hid_copy.wait()
    for k in range(2):
        act_edge(result, k).wait_send()
    each(R - 1, lambda k: lead_copy(lead.at[r], (r + k + 1) % R).wait_send())
    for i in range(G):
        each(R - 1, lambda k: part_copy(i, (r + k + 1) % R).wait_send())
    each(C - 1, lambda k: col_copy(k).wait_send())

    @pl.when(even)
    def _():
        each(R * C - 1, lambda k: stat_copy(k).wait_send())
        each(C - 1, lambda k: mom_copy(k).wait_send())


def write_out(a, b, c, a_out, b_out, c_out, sem):
    pairs = ((a, a_out), (b, b_out), (c, c_out))
    copies = [pltpu.make_async_copy(i, o, sem.at[k]) for k, (i, o) in enumerate(pairs)]
    for copy in copies:
        copy.start()
    for copy in copies:
        copy.wait()


def per_device(S, R, C, *arguments):
    act_in, hid_in, grad_in, saved_in, saved_pre, weights, norm_gain, norm_bias = arguments
    own, DC = act_in.shape[1:]
    T, F = hid_in.shape[1:]
    N = 8
    bf16, f32 = jnp.bfloat16, jnp.float32
    dma = pltpu.SemaphoreType.DMA
    scratch = [
        pltpu.VMEM((DC, F), bf16),
        pltpu.VMEM((R, own, DC), bf16),
        pltpu.VMEM((own, DC), bf16),
        pltpu.VMEM((own, DC), bf16),
        pltpu.VMEM((T, F), bf16),
        pltpu.VMEM((T, F), bf16),
        pltpu.VMEM(norm_gain.shape, f32),
        pltpu.VMEM(norm_bias.shape, f32),
        pltpu.VMEM((T, F), bf16),
        pltpu.VMEM((T, DC), f32),
        pltpu.VMEM((T, LANES), f32),
        pltpu.VMEM((T, LANES), f32),
        pltpu.VMEM((R * C, 4, own, LANES), f32),
        pltpu.VMEM((R, own, DC), f32),
        pltpu.VMEM((R, own, DC), f32),
        pltpu.VMEM((C, T, F), f32),
        pltpu.VMEM((C, 2, own, LANES), f32),
        pltpu.VMEM((T, F), bf16),
        pltpu.VMEM((own, DC), bf16),
        dma((N,)), dma((7,)),
        dma((R,)), dma((R,)),
        dma((R * C,)), dma((R * C,)),
        dma((N // 2, R)), dma((N // 2, R)),
        dma((C,)), dma((C,)),
        dma((C,)), dma((C,)),
        dma((3,)), dma((3,)),
    ]
    flops = 4 * T * F * DC
    moved = 2 * DC * F
    results = pl.pallas_call(
        functools.partial(kernel, (S, R, C, own, T, F, DC, N)),
        out_shape=[
            pltpu.VMEM(act_in.shape, bf16),
            pltpu.VMEM(hid_in.shape, bf16),
            pltpu.VMEM(grad_in.shape, bf16),
        ],
        in_specs=[pl.BlockSpec(memory_space=pl.ANY)] * 8,
        out_specs=[pl.BlockSpec(memory_space=pl.ANY)] * 3,
        scratch_shapes=scratch,
        compiler_params=pltpu.CompilerParams(
            collective_id=0, has_side_effects=True, vmem_limit_bytes=LIMIT
        ),
        cost_estimate=pl.CostEstimate(flops=flops, bytes_accessed=moved, transcendentals=T * F),
    )(*(pltpu.with_memory_space_constraint(a, pltpu.HBM) for a in arguments))
    return pl.pallas_call(
        write_out,
        out_shape=[jax.ShapeDtypeStruct(a.shape, a.dtype) for a in results],
        in_specs=[pl.BlockSpec(memory_space=pl.ANY)] * 3,
        out_specs=[pl.BlockSpec(memory_space=pl.ANY)] * 3,
        scratch_shapes=[dma((3,))],
        compiler_params=pltpu.CompilerParams(vmem_limit_bytes=LIMIT),
    )(*results)


def solution(mesh):
    S, R, C = (mesh.shape[name] for name in ("section", "row", "col"))
    in_specs = (
        P("section", "row", "col"),
        P("section", None, "row"),
        P("section", "row", "col"),
        P("section", "row", "col"),
        P("section", None, "row"),
        P("section", "col", "row"),
        P(None, "col"),
        P(None, "col"),
    )
    out_specs = (P("section", "row", "col"), P("section", None, "row"), P("section", "row", "col"))
    return jax.shard_map(
        functools.partial(per_device, S, R, C),
        mesh=mesh, in_specs=in_specs, out_specs=out_specs, check_vma=False,
    )
```

```python
import functools

import jax
import jax.numpy as jnp
from jax import lax
from jax.experimental import pallas as pl
from jax.experimental.pallas import tpu as pltpu
from jax.sharding import PartitionSpec as P

EPSILON = 1e-05
ROOT = 0.7978845608028654
CUBIC = 0.044715
MESH = pl.DeviceIdType.MESH
LANES = 128
LIMIT = 48 * 2**20


def each(count, body):
    if count <= 8:
        for step in range(count):
            body(step)
    else:
        lax.fori_loop(0, count, lambda step, carry: (body(step), carry)[1], 0)


def gelu(x):
    return x * (0.5 * (1.0 + jnp.tanh(ROOT * (x + CUBIC * (x * x * x)))))


def gelu_slope(x):
    t = jnp.tanh(ROOT * (x + CUBIC * (x * x * x)))
    return 0.5 * (1.0 + t) + 0.5 * x * (1.0 - t * t) * (ROOT * (1.0 + 3.0 * CUBIC * (x * x)))


def row_sum(values):
    return jnp.broadcast_to(jnp.sum(values, axis=-1, keepdims=True), (values.shape[0], LANES))


def kernel(
    sizes,
    act_in, hid_in, grad_in, saved_in, pre_in, weights, gain_in, bias_in,
    act_out, hid_out, grad_out,
    w, lead, other, saved, hid, pre, gain, bias, right, x, mean, scale, stats,
    parts, sums, partial, moments, hidden, result,
    w_sem, local_sem, lead_send, lead_recv, stat_send, stat_recv, part_send, part_recv,
    col_send, col_recv, mom_send, mom_recv, edge_send, edge_recv,
):
    S, R, C, own, T, F, DC, N = sizes
    D = DC * C
    K = DC // N
    s, r, c = lax.axis_index("section"), lax.axis_index("row"), lax.axis_index("col")
    even = s % 2 == 0
    odd = s % 2 == 1
    layer = s // 2
    up, down = (s + 1) % S, (s + S - 1) % S
    me = r * C + c

    def local(src, dst, k):
        return pltpu.make_async_copy(src, dst, local_sem.at[k])

    def remote(src, dst, send, recv, **device):
        return pltpu.make_async_remote_copy(
            src_ref=src, dst_ref=dst, send_sem=send, recv_sem=recv,
            device_id=device, device_id_type=MESH,
        )

    barrier = pltpu.get_barrier_semaphore()
    for neighbour in (up, down):
        pl.semaphore_signal(barrier, inc=1, device_id={"section": neighbour}, device_id_type=MESH)

    def place(k):
        to = (me + k + 1) % (R * C)
        return to, {"row": to // C, "col": to % C}

    def greet(k):
        pl.semaphore_signal(barrier, inc=1, device_id=place(k)[1], device_id_type=MESH)

    each(R * C - 1, greet)

    @pl.when(even)
    def _():
        local(act_in.at[0], lead.at[r], 0).start()
        local(grad_in.at[0], other, 1).start()

    @pl.when(odd)
    def _():
        local(grad_in.at[0], lead.at[r], 0).start()
        local(act_in.at[0], other, 1).start()

    local_saved = local(saved_in.at[0], saved, 2)
    local_hid, local_pre = local(hid_in.at[0], hid, 3), local(pre_in.at[0], pre, 4)
    local_gain, local_bias = local(gain_in, gain, 5), local(bias_in, bias, 6)
    for copy in (local_saved, local_hid, local_pre):
        copy.start()

    def weight_copy(i):
        rows = pl.ds(i * K, K)
        return pltpu.make_async_copy(weights.at[0, rows], w.at[rows], w_sem.at[i])

    for i in range(N):
        weight_copy(i).start()
    local_gain.start()
    local_bias.start()

    pl.semaphore_wait(barrier, R * C + 1)

    def lead_copy(src, to):
        return remote(src, lead.at[r], lead_send.at[to], lead_recv.at[r], row=to)

    @pl.when(even)
    def _():
        each(R - 1, lambda k: lead_copy(act_in.at[0], (r + k + 1) % R).start())

    @pl.when(odd)
    def _():
        each(R - 1, lambda k: lead_copy(grad_in.at[0], (r + k + 1) % R).start())

    def stat_copy(k):
        to, device = place(k)
        return remote(stats.at[me], stats.at[me], stat_send.at[to], stat_recv.at[me], **device)

    local(act_in.at[0], lead.at[r], 0).wait()
    local_saved.wait()

    @pl.when(even)
    def _():
        v = lead[r].astype(jnp.float32)
        z = saved[...].astype(jnp.float32)
        stats[me, 0] = row_sum(v)
        stats[me, 1] = row_sum(v * v)
        stats[me, 2] = row_sum(z)
        stats[me, 3] = row_sum(z * z)
        each(R * C - 1, lambda k: stat_copy(k).start())

    local_hid.wait()
    local_pre.wait()

    def act_edge(src, k):
        return remote(src, act_out.at[0], edge_send.at[k], edge_recv.at[0], section=up)

    def grad_edge(src, k):
        return remote(src, grad_out.at[0], edge_send.at[k], edge_recv.at[1], section=down)

    def spread(rows):
        extra = right.shape[0] - T
        if extra:
            rows = jnp.concatenate([rows, jnp.zeros((extra, F), jnp.float32)], axis=0)
        right[...] = rows.astype(jnp.bfloat16)

    @pl.when(even)
    def _():
        act_edge(lead.at[r], 0).start()
        h = hid[...].astype(jnp.float32)
        spread(h * gelu_slope(pre[...].astype(jnp.float32)))

    @pl.when(odd)
    def _():
        grad_edge(lead.at[r], 0).start()
        spread(hid[...].astype(jnp.float32))

    G = N // 2
    wide = DC // G

    def part_copy(i, to):
        columns = pl.ds(i * wide, wide)
        return remote(
            parts.at[to, :, columns], sums.at[r, :, columns],
            part_send.at[i, to], part_recv.at[i, r], row=to,
        )

    for i in range(N):
        weight_copy(i).wait()
        tall = lax.dot_general(
            w[i * K:(i + 1) * K, :], right[...], (((1,), (1,)), ((), ())),
            preferred_element_type=jnp.float32,
        )
        term = tall.T[:T]
        for q in range(R):
            parts[q, :, i * K:(i + 1) * K] = term[q * own:(q + 1) * own, :]
        if i % 2 == 1:
            each(R - 1, lambda k: part_copy(i // 2, (r + k + 1) % R).start())

    def lead_arrived(k):
        q = (r + k + 1) % R
        remote(lead.at[q], lead.at[q], lead_send.at[q], lead_recv.at[q], row=q).wait_recv()

    each(R - 1, lead_arrived)

    def stat_arrived(k):
        q, device = place(k)
        remote(stats.at[q], stats.at[q], stat_send.at[q], stat_recv.at[q], **device).wait_recv()

    def factors(q, first):
        total, squares = stats[q * C, first], stats[q * C, first + 1]
        for j in range(1, C):
            total = total + stats[q * C + j, first]
            squares = squares + stats[q * C + j, first + 1]
        average = total / D
        return average, lax.rsqrt(squares / D - average * average + EPSILON)

    @pl.when(even)
    def _():
        each(R * C - 1, stat_arrived)
        for q in range(R):
            rows = slice(q * own, (q + 1) * own)
            average, inverse = factors(q, 0)
            mean[rows, :] = average
            scale[rows, :] = inverse

    for q in range(R):
        x[q * own:(q + 1) * own, :] = lead[q].astype(jnp.float32)

    local(act_in.at[0], other, 1).wait()
    local_gain.wait()
    local_bias.wait()

    def dot(a, b):
        return jnp.dot(a.astype(jnp.bfloat16), b, preferred_element_type=jnp.float32)

    def half(first):
        span = DC // 2
        base, cut = first * span, F // 256 * 256

        def product(left):
            if F - cut != LANES or span % 512:
                return dot(left, w[base:base + span, :])
            main = dot(left, w[base:base + span, :cut])
            middle = span // 2
            stacked = jnp.concatenate([left[:, :middle], left[:, middle:]], axis=0)
            beside = jnp.concatenate(
                [w[base:base + middle, cut:], w[base + middle:base + span, cut:]], axis=1
            )
            both = dot(stacked, beside)
            return jnp.concatenate([main, both[:T, :LANES] + both[T:, LANES:]], axis=1)

        def keep(total):
            partial[c] = total if first == 0 else partial[c] + total

        columns = slice(base, base + span)

        @pl.when(even)
        def _():
            m, f = mean[:, :1], scale[:, :1]

            g, b = gain[pl.ds(layer, 1), columns], bias[pl.ds(layer, 1), columns]
            keep(product((x[:, columns] - m) * f * g + b))

        @pl.when(odd)
        def _():
            keep(product(x[:, columns]))

    half(0)

    def col_copy(k):
        to = (c + k + 1) % C
        return remote(partial.at[c], partial.at[c], col_send.at[to], col_recv.at[c], col=to)

    def part_arrived(k):
        q = (r + k + 1) % R
        for i in range(G):
            columns = pl.ds(i * wide, wide)
            remote(
                parts.at[q, :, columns], sums.at[q, :, columns],
                part_send.at[i, q], part_recv.at[i, q], row=q,
            ).wait_recv()

    each(R - 1, part_arrived)
    sums[r] = parts[r]
    term = sums[0]
    for q in range(1, R):
        term = term + sums[q]

    @pl.when(odd)
    def _():
        result[...] = (other[...].astype(jnp.float32) + term).astype(jnp.bfloat16)
        act_edge(result, 1).start()

    def mom_copy(k):
        to = (c + k + 1) % C
        return remote(moments.at[c], moments.at[c], mom_send.at[to], mom_recv.at[c], col=to)

    def saved_hat():
        average, inverse = factors(r, 2)
        return (saved[...].astype(jnp.float32) - average[:, :1]) * inverse[:, :1], inverse[:, :1]

    @pl.when(even)
    def _():
        scaled = term * gain[pl.ds(layer, 1), :]
        sums[0] = scaled
        moments[c, 0] = row_sum(scaled)
        moments[c, 1] = row_sum(scaled * saved_hat()[0])
        each(C - 1, lambda k: mom_copy(k).start())

    half(1)
    each(C - 1, lambda k: col_copy(k).start())

    @pl.when(even)
    def _():
        def mom_arrived(k):
            q = (c + k + 1) % C
            remote(moments.at[q], moments.at[q], mom_send.at[q], mom_recv.at[q], col=q).wait_recv()

        each(C - 1, mom_arrived)
        first, second = moments[0, 0], moments[0, 1]
        for q in range(1, C):
            first = first + moments[q, 0]
            second = second + moments[q, 1]
        first, second = first[:, :1] / D, second[:, :1] / D
        h, inverse = saved_hat()
        moved = other[...].astype(jnp.float32) + inverse * (sums[0] - first - h * second)
        result[...] = moved.astype(jnp.bfloat16)
        grad_edge(result, 1).start()

    def col_arrived(k):
        q = (c + k + 1) % C
        remote(partial.at[q], partial.at[q], col_send.at[q], col_recv.at[q], col=q).wait_recv()

    each(C - 1, col_arrived)
    summed = partial[0]
    for q in range(1, C):
        summed = summed + partial[q]

    @pl.when(even)
    def _():
        hidden[...] = gelu(summed).astype(jnp.bfloat16)

    @pl.when(odd)
    def _():
        hidden[...] = summed.astype(jnp.bfloat16)

    pair = s + 1 - 2 * (s % 2)
    hid_copy = remote(hidden, hid_out.at[0], edge_send.at[2], edge_recv.at[2], section=pair)
    hid_copy.start()

    act_edge(result, 0).wait_recv()
    grad_edge(result, 0).wait_recv()
    hid_copy.wait()
    for k in range(2):
        act_edge(result, k).wait_send()
    each(R - 1, lambda k: lead_copy(lead.at[r], (r + k + 1) % R).wait_send())
    for i in range(G):
        each(R - 1, lambda k: part_copy(i, (r + k + 1) % R).wait_send())
    each(C - 1, lambda k: col_copy(k).wait_send())

    @pl.when(even)
    def _():
        each(R * C - 1, lambda k: stat_copy(k).wait_send())
        each(C - 1, lambda k: mom_copy(k).wait_send())


def write_out(a, b, c, a_out, b_out, c_out, sem):
    pairs = ((a, a_out), (b, b_out), (c, c_out))
    copies = [pltpu.make_async_copy(i, o, sem.at[k]) for k, (i, o) in enumerate(pairs)]
    for copy in copies:
        copy.start()
    for copy in copies:
        copy.wait()


def per_device(S, R, C, *arguments):
    act_in, hid_in, grad_in, saved_in, saved_pre, weights, norm_gain, norm_bias = arguments
    own, DC = act_in.shape[1:]
    T, F = hid_in.shape[1:]
    N = 8
    bf16, f32 = jnp.bfloat16, jnp.float32
    dma = pltpu.SemaphoreType.DMA
    scratch = [
        pltpu.VMEM((DC, F), bf16),
        pltpu.VMEM((R, own, DC), bf16),
        pltpu.VMEM((own, DC), bf16),
        pltpu.VMEM((own, DC), bf16),
        pltpu.VMEM((T, F), bf16),
        pltpu.VMEM((T, F), bf16),
        pltpu.VMEM(norm_gain.shape, f32),
        pltpu.VMEM(norm_bias.shape, f32),
        pltpu.VMEM(((T + LANES - 1) // LANES * LANES, F), bf16),
        pltpu.VMEM((T, DC), f32),
        pltpu.VMEM((T, LANES), f32),
        pltpu.VMEM((T, LANES), f32),
        pltpu.VMEM((R * C, 4, own, LANES), f32),
        pltpu.VMEM((R, own, DC), f32),
        pltpu.VMEM((R, own, DC), f32),
        pltpu.VMEM((C, T, F), f32),
        pltpu.VMEM((C, 2, own, LANES), f32),
        pltpu.VMEM((T, F), bf16),
        pltpu.VMEM((own, DC), bf16),
        dma((N,)), dma((7,)),
        dma((R,)), dma((R,)),
        dma((R * C,)), dma((R * C,)),
        dma((N // 2, R)), dma((N // 2, R)),
        dma((C,)), dma((C,)),
        dma((C,)), dma((C,)),
        dma((3,)), dma((3,)),
    ]
    flops = 4 * T * F * DC
    moved = 2 * DC * F
    results = pl.pallas_call(
        functools.partial(kernel, (S, R, C, own, T, F, DC, N)),
        out_shape=[
            pltpu.VMEM(act_in.shape, bf16),
            pltpu.VMEM(hid_in.shape, bf16),
            pltpu.VMEM(grad_in.shape, bf16),
        ],
        in_specs=[pl.BlockSpec(memory_space=pl.ANY)] * 8,
        out_specs=[pl.BlockSpec(memory_space=pl.ANY)] * 3,
        scratch_shapes=scratch,
        compiler_params=pltpu.CompilerParams(
            collective_id=0, has_side_effects=True, vmem_limit_bytes=LIMIT
        ),
        cost_estimate=pl.CostEstimate(flops=flops, bytes_accessed=moved, transcendentals=T * F),
    )(*(pltpu.with_memory_space_constraint(a, pltpu.HBM) for a in arguments))
    return pl.pallas_call(
        write_out,
        out_shape=[jax.ShapeDtypeStruct(a.shape, a.dtype) for a in results],
        in_specs=[pl.BlockSpec(memory_space=pl.ANY)] * 3,
        out_specs=[pl.BlockSpec(memory_space=pl.ANY)] * 3,
        scratch_shapes=[dma((3,))],
        compiler_params=pltpu.CompilerParams(vmem_limit_bytes=LIMIT),
    )(*results)


def solution(mesh):
    S, R, C = (mesh.shape[name] for name in ("section", "row", "col"))
    in_specs = (
        P("section", "row", "col"),
        P("section", None, "row"),
        P("section", "row", "col"),
        P("section", "row", "col"),
        P("section", None, "row"),
        P("section", "col", "row"),
        P(None, "col"),
        P(None, "col"),
    )
    out_specs = (P("section", "row", "col"), P("section", None, "row"), P("section", "row", "col"))
    return jax.shard_map(
        functools.partial(per_device, S, R, C),
        mesh=mesh, in_specs=in_specs, out_specs=out_specs, check_vma=False,
    )
```

```python
import functools

import jax
import jax.numpy as jnp
from jax import lax
from jax.experimental import pallas as pl
from jax.experimental.pallas import tpu as pltpu
from jax.sharding import PartitionSpec as P

EPSILON = 1e-05
ROOT = 0.7978845608028654
CUBIC = 0.044715
MESH = pl.DeviceIdType.MESH
LANES = 128
LIMIT = 48 * 2**20


def each(count, body):
    if count <= 8:
        for step in range(count):
            body(step)
    else:
        lax.fori_loop(0, count, lambda step, carry: (body(step), carry)[1], 0)


def gelu(x):
    return x * (0.5 * (1.0 + jnp.tanh(ROOT * (x + CUBIC * (x * x * x)))))


def gelu_slope(x):
    t = jnp.tanh(ROOT * (x + CUBIC * (x * x * x)))
    return 0.5 * (1.0 + t) + 0.5 * x * (1.0 - t * t) * (ROOT * (1.0 + 3.0 * CUBIC * (x * x)))


def row_sum(values):
    return jnp.broadcast_to(jnp.sum(values, axis=-1, keepdims=True), (values.shape[0], LANES))


def kernel(
    sizes,
    act_in, hid_in, grad_in, saved_in, pre_in, weights, gain_in, bias_in,
    act_out, hid_out, grad_out,
    w, lead, other, saved, hid, pre, gain, bias, right, last_right, x, mean, scale, stats,
    parts, sums, partial, moments, hidden, result,
    w_sem, local_sem, lead_send, lead_recv, stat_send, stat_recv, part_send, part_recv,
    col_send, col_recv, mom_send, mom_recv, edge_send, edge_recv,
):
    S, R, C, own, T, F, DC, N = sizes
    D = DC * C
    K = DC // N
    s, r, c = lax.axis_index("section"), lax.axis_index("row"), lax.axis_index("col")
    even = s % 2 == 0
    odd = s % 2 == 1
    layer = s // 2
    up, down = (s + 1) % S, (s + S - 1) % S
    me = r * C + c

    def local(src, dst, k):
        return pltpu.make_async_copy(src, dst, local_sem.at[k])

    def remote(src, dst, send, recv, **device):
        return pltpu.make_async_remote_copy(
            src_ref=src, dst_ref=dst, send_sem=send, recv_sem=recv,
            device_id=device, device_id_type=MESH,
        )

    barrier = pltpu.get_barrier_semaphore()
    for neighbour in (up, down):
        pl.semaphore_signal(barrier, inc=1, device_id={"section": neighbour}, device_id_type=MESH)

    def place(k):
        to = (me + k + 1) % (R * C)
        return to, {"row": to // C, "col": to % C}

    def greet(k):
        pl.semaphore_signal(barrier, inc=1, device_id=place(k)[1], device_id_type=MESH)

    each(R * C - 1, greet)

    @pl.when(even)
    def _():
        local(act_in.at[0], lead.at[r], 0).start()
        local(grad_in.at[0], other, 1).start()

    @pl.when(odd)
    def _():
        local(grad_in.at[0], lead.at[r], 0).start()
        local(act_in.at[0], other, 1).start()

    local_saved = local(saved_in.at[0], saved, 2)
    local_hid, local_pre = local(hid_in.at[0], hid, 3), local(pre_in.at[0], pre, 4)
    local_gain, local_bias = local(gain_in, gain, 5), local(bias_in, bias, 6)
    for copy in (local_saved, local_hid, local_pre):
        copy.start()

    def weight_copy(i):
        rows = pl.ds(i * K, K)
        return pltpu.make_async_copy(weights.at[0, rows], w.at[rows], w_sem.at[i])

    for i in range(N):
        weight_copy(i).start()
    local_gain.start()
    local_bias.start()

    pl.semaphore_wait(barrier, R * C + 1)

    def lead_copy(src, to):
        return remote(src, lead.at[r], lead_send.at[to], lead_recv.at[r], row=to)

    @pl.when(even)
    def _():
        each(R - 1, lambda k: lead_copy(act_in.at[0], (r + k + 1) % R).start())

    @pl.when(odd)
    def _():
        each(R - 1, lambda k: lead_copy(grad_in.at[0], (r + k + 1) % R).start())

    def stat_copy(k):
        to, device = place(k)
        return remote(stats.at[me], stats.at[me], stat_send.at[to], stat_recv.at[me], **device)

    local(act_in.at[0], lead.at[r], 0).wait()
    local_saved.wait()

    @pl.when(even)
    def _():
        v = lead[r].astype(jnp.float32)
        z = saved[...].astype(jnp.float32)
        stats[me, 0] = row_sum(v)
        stats[me, 1] = row_sum(v * v)
        stats[me, 2] = row_sum(z)
        stats[me, 3] = row_sum(z * z)
        each(R * C - 1, lambda k: stat_copy(k).start())

    local_hid.wait()
    local_pre.wait()

    def act_edge(src, k):
        return remote(src, act_out.at[0], edge_send.at[k], edge_recv.at[0], section=up)

    def grad_edge(src, k):
        return remote(src, grad_out.at[0], edge_send.at[k], edge_recv.at[1], section=down)

    cut = F // 256 * 256
    pack = F - cut == LANES and DC % 2048 == 0
    wide = DC // (N // 2)

    def spread(rows):
        right[...] = rows.astype(jnp.bfloat16)
        if pack:
            last, none = rows[:, cut:], jnp.zeros((T, LANES), jnp.float32)
            upper = jnp.concatenate([last, none], axis=1)
            lower = jnp.concatenate([none, last], axis=1)
            last_right[...] = jnp.concatenate([upper, lower], axis=0).astype(jnp.bfloat16)

    @pl.when(even)
    def _():
        act_edge(lead.at[r], 0).start()
        h = hid[...].astype(jnp.float32)
        spread(h * gelu_slope(pre[...].astype(jnp.float32)))

    @pl.when(odd)
    def _():
        grad_edge(lead.at[r], 0).start()
        spread(hid[...].astype(jnp.float32))

    G = N // 2

    def part_copy(i, to):
        columns = pl.ds(i * wide, wide)
        return remote(
            parts.at[to, :, columns], sums.at[r, :, columns],
            part_send.at[i, to], part_recv.at[i, r], row=to,
        )

    def across(a, b):
        return lax.dot_general(
            a, b, (((1,), (1,)), ((), ())), preferred_element_type=jnp.float32
        )

    for i in range(G):
        weight_copy(2 * i).wait()
        weight_copy(2 * i + 1).wait()
        low, high = i * wide, (i + 1) * wide
        middle = low + wide // 2
        if pack:
            beside = jnp.concatenate([w[low:middle, cut:], w[middle:high, cut:]], axis=1)
            both = across(last_right[...], beside)
            term = across(right[:, :cut], w[low:high, :cut])
            term = term + jnp.concatenate([both[:T], both[T:]], axis=1)
        else:
            term = across(right[...], w[low:high, :])
        for q in range(R):
            parts[q, :, low:high] = term[q * own:(q + 1) * own, :]
        each(R - 1, lambda k: part_copy(i, (r + k + 1) % R).start())

    def lead_arrived(k):
        q = (r + k + 1) % R
        remote(lead.at[q], lead.at[q], lead_send.at[q], lead_recv.at[q], row=q).wait_recv()

    each(R - 1, lead_arrived)

    def stat_arrived(k):
        q, device = place(k)
        remote(stats.at[q], stats.at[q], stat_send.at[q], stat_recv.at[q], **device).wait_recv()

    def factors(q, first):
        total, squares = stats[q * C, first], stats[q * C, first + 1]
        for j in range(1, C):
            total = total + stats[q * C + j, first]
            squares = squares + stats[q * C + j, first + 1]
        average = total / D
        return average, lax.rsqrt(squares / D - average * average + EPSILON)

    @pl.when(even)
    def _():
        each(R * C - 1, stat_arrived)
        for q in range(R):
            rows = slice(q * own, (q + 1) * own)
            average, inverse = factors(q, 0)
            mean[rows, :] = average
            scale[rows, :] = inverse

    for q in range(R):
        x[q * own:(q + 1) * own, :] = lead[q].astype(jnp.float32)

    local(act_in.at[0], other, 1).wait()
    local_gain.wait()
    local_bias.wait()

    def dot(a, b):
        return jnp.dot(a.astype(jnp.bfloat16), b, preferred_element_type=jnp.float32)

    def half(first):
        span = DC // 2
        base = first * span

        def product(left):
            if not pack:
                return dot(left, w[base:base + span, :])
            main = dot(left, w[base:base + span, :cut])
            middle = span // 2
            stacked = jnp.concatenate([left[:, :middle], left[:, middle:]], axis=0)
            beside = jnp.concatenate(
                [w[base:base + middle, cut:], w[base + middle:base + span, cut:]], axis=1
            )
            both = dot(stacked, beside)
            return jnp.concatenate([main, both[:T, :LANES] + both[T:, LANES:]], axis=1)

        def keep(total):
            partial[c] = total if first == 0 else partial[c] + total

        columns = slice(base, base + span)

        @pl.when(even)
        def _():
            m, f = mean[:, :1], scale[:, :1]

            g, b = gain[pl.ds(layer, 1), columns], bias[pl.ds(layer, 1), columns]
            keep(product((x[:, columns] - m) * f * g + b))

        @pl.when(odd)
        def _():
            keep(product(x[:, columns]))

    half(0)

    def col_copy(k):
        to = (c + k + 1) % C
        return remote(partial.at[c], partial.at[c], col_send.at[to], col_recv.at[c], col=to)

    def part_arrived(k):
        q = (r + k + 1) % R
        for i in range(G):
            columns = pl.ds(i * wide, wide)
            remote(
                parts.at[q, :, columns], sums.at[q, :, columns],
                part_send.at[i, q], part_recv.at[i, q], row=q,
            ).wait_recv()

    each(R - 1, part_arrived)
    sums[r] = parts[r]
    term = sums[0]
    for q in range(1, R):
        term = term + sums[q]

    @pl.when(odd)
    def _():
        result[...] = (other[...].astype(jnp.float32) + term).astype(jnp.bfloat16)
        act_edge(result, 1).start()

    def mom_copy(k):
        to = (c + k + 1) % C
        return remote(moments.at[c], moments.at[c], mom_send.at[to], mom_recv.at[c], col=to)

    def saved_hat():
        average, inverse = factors(r, 2)
        return (saved[...].astype(jnp.float32) - average[:, :1]) * inverse[:, :1], inverse[:, :1]

    @pl.when(even)
    def _():
        scaled = term * gain[pl.ds(layer, 1), :]
        sums[0] = scaled
        moments[c, 0] = row_sum(scaled)
        moments[c, 1] = row_sum(scaled * saved_hat()[0])
        each(C - 1, lambda k: mom_copy(k).start())

    half(1)
    each(C - 1, lambda k: col_copy(k).start())

    @pl.when(even)
    def _():
        def mom_arrived(k):
            q = (c + k + 1) % C
            remote(moments.at[q], moments.at[q], mom_send.at[q], mom_recv.at[q], col=q).wait_recv()

        each(C - 1, mom_arrived)
        first, second = moments[0, 0], moments[0, 1]
        for q in range(1, C):
            first = first + moments[q, 0]
            second = second + moments[q, 1]
        first, second = first[:, :1] / D, second[:, :1] / D
        h, inverse = saved_hat()
        moved = other[...].astype(jnp.float32) + inverse * (sums[0] - first - h * second)
        result[...] = moved.astype(jnp.bfloat16)
        grad_edge(result, 1).start()

    def col_arrived(k):
        q = (c + k + 1) % C
        remote(partial.at[q], partial.at[q], col_send.at[q], col_recv.at[q], col=q).wait_recv()

    each(C - 1, col_arrived)
    summed = partial[0]
    for q in range(1, C):
        summed = summed + partial[q]

    @pl.when(even)
    def _():
        hidden[...] = gelu(summed).astype(jnp.bfloat16)

    @pl.when(odd)
    def _():
        hidden[...] = summed.astype(jnp.bfloat16)

    pair = s + 1 - 2 * (s % 2)
    hid_copy = remote(hidden, hid_out.at[0], edge_send.at[2], edge_recv.at[2], section=pair)
    hid_copy.start()

    act_edge(result, 0).wait_recv()
    grad_edge(result, 0).wait_recv()
    hid_copy.wait()
    for k in range(2):
        act_edge(result, k).wait_send()
    each(R - 1, lambda k: lead_copy(lead.at[r], (r + k + 1) % R).wait_send())
    for i in range(G):
        each(R - 1, lambda k: part_copy(i, (r + k + 1) % R).wait_send())
    each(C - 1, lambda k: col_copy(k).wait_send())

    @pl.when(even)
    def _():
        each(R * C - 1, lambda k: stat_copy(k).wait_send())
        each(C - 1, lambda k: mom_copy(k).wait_send())


def write_out(a, b, c, a_out, b_out, c_out, sem):
    pairs = ((a, a_out), (b, b_out), (c, c_out))
    copies = [pltpu.make_async_copy(i, o, sem.at[k]) for k, (i, o) in enumerate(pairs)]
    for copy in copies:
        copy.start()
    for copy in copies:
        copy.wait()


def per_device(S, R, C, *arguments):
    act_in, hid_in, grad_in, saved_in, saved_pre, weights, norm_gain, norm_bias = arguments
    own, DC = act_in.shape[1:]
    T, F = hid_in.shape[1:]
    N = 8
    bf16, f32 = jnp.bfloat16, jnp.float32
    dma = pltpu.SemaphoreType.DMA
    scratch = [
        pltpu.VMEM((DC, F), bf16),
        pltpu.VMEM((R, own, DC), bf16),
        pltpu.VMEM((own, DC), bf16),
        pltpu.VMEM((own, DC), bf16),
        pltpu.VMEM((T, F), bf16),
        pltpu.VMEM((T, F), bf16),
        pltpu.VMEM(norm_gain.shape, f32),
        pltpu.VMEM(norm_bias.shape, f32),
        pltpu.VMEM((T, F), bf16),
        pltpu.VMEM((2 * T, 2 * LANES), bf16),
        pltpu.VMEM((T, DC), f32),
        pltpu.VMEM((T, LANES), f32),
        pltpu.VMEM((T, LANES), f32),
        pltpu.VMEM((R * C, 4, own, LANES), f32),
        pltpu.VMEM((R, own, DC), f32),
        pltpu.VMEM((R, own, DC), f32),
        pltpu.VMEM((C, T, F), f32),
        pltpu.VMEM((C, 2, own, LANES), f32),
        pltpu.VMEM((T, F), bf16),
        pltpu.VMEM((own, DC), bf16),
        dma((N,)), dma((7,)),
        dma((R,)), dma((R,)),
        dma((R * C,)), dma((R * C,)),
        dma((N // 2, R)), dma((N // 2, R)),
        dma((C,)), dma((C,)),
        dma((C,)), dma((C,)),
        dma((3,)), dma((3,)),
    ]
    flops = 4 * T * F * DC
    moved = 2 * DC * F
    results = pl.pallas_call(
        functools.partial(kernel, (S, R, C, own, T, F, DC, N)),
        out_shape=[
            pltpu.VMEM(act_in.shape, bf16),
            pltpu.VMEM(hid_in.shape, bf16),
            pltpu.VMEM(grad_in.shape, bf16),
        ],
        in_specs=[pl.BlockSpec(memory_space=pl.ANY)] * 8,
        out_specs=[pl.BlockSpec(memory_space=pl.ANY)] * 3,
        scratch_shapes=scratch,
        compiler_params=pltpu.CompilerParams(
            collective_id=0, has_side_effects=True, vmem_limit_bytes=LIMIT
        ),
        cost_estimate=pl.CostEstimate(flops=flops, bytes_accessed=moved, transcendentals=T * F),
    )(*(pltpu.with_memory_space_constraint(a, pltpu.HBM) for a in arguments))
    return pl.pallas_call(
        write_out,
        out_shape=[jax.ShapeDtypeStruct(a.shape, a.dtype) for a in results],
        in_specs=[pl.BlockSpec(memory_space=pl.ANY)] * 3,
        out_specs=[pl.BlockSpec(memory_space=pl.ANY)] * 3,
        scratch_shapes=[dma((3,))],
        compiler_params=pltpu.CompilerParams(vmem_limit_bytes=LIMIT),
    )(*results)


def solution(mesh):
    S, R, C = (mesh.shape[name] for name in ("section", "row", "col"))
    in_specs = (
        P("section", "row", "col"),
        P("section", None, "row"),
        P("section", "row", "col"),
        P("section", "row", "col"),
        P("section", None, "row"),
        P("section", "col", "row"),
        P(None, "col"),
        P(None, "col"),
    )
    out_specs = (P("section", "row", "col"), P("section", None, "row"), P("section", "row", "col"))
    return jax.shard_map(
        functools.partial(per_device, S, R, C),
        mesh=mesh, in_specs=in_specs, out_specs=out_specs, check_vma=False,
    )
```

```python
import functools

import jax
import jax.numpy as jnp
from jax import lax
from jax.experimental import pallas as pl
from jax.experimental.pallas import tpu as pltpu
from jax.sharding import PartitionSpec as P

EPSILON = 1e-05
ROOT = 0.7978845608028654
CUBIC = 0.044715
MESH = pl.DeviceIdType.MESH
LANES = 128
LIMIT = 48 * 2**20


def each(count, body):
    if count <= 8:
        for step in range(count):
            body(step)
    else:
        lax.fori_loop(0, count, lambda step, carry: (body(step), carry)[1], 0)


def gelu(x):
    return x * (0.5 * (1.0 + jnp.tanh(ROOT * (x + CUBIC * (x * x * x)))))


def gelu_slope(x):
    t = jnp.tanh(ROOT * (x + CUBIC * (x * x * x)))
    return 0.5 * (1.0 + t) + 0.5 * x * (1.0 - t * t) * (ROOT * (1.0 + 3.0 * CUBIC * (x * x)))


def row_sum(values):
    return jnp.broadcast_to(jnp.sum(values, axis=-1, keepdims=True), (values.shape[0], LANES))


def kernel(
    sizes,
    act_in, hid_in, grad_in, saved_in, pre_in, weights, gain_in, bias_in,
    act_out, hid_out, grad_out,
    w, lead, other, saved, hid, pre, gain, bias, right, last_right, x, mean, scale, stats,
    parts, sums, partial, moments, hidden, result,
    w_sem, local_sem, lead_send, lead_recv, stat_send, stat_recv, part_send, part_recv,
    col_send, col_recv, mom_send, mom_recv, edge_send, edge_recv,
):
    S, R, C, own, T, F, DC, N = sizes
    D = DC * C
    K = DC // N
    s, r, c = lax.axis_index("section"), lax.axis_index("row"), lax.axis_index("col")
    even = s % 2 == 0
    odd = s % 2 == 1
    layer = s // 2
    up, down = (s + 1) % S, (s + S - 1) % S
    me = r * C + c

    def local(src, dst, k):
        return pltpu.make_async_copy(src, dst, local_sem.at[k])

    def remote(src, dst, send, recv, **device):
        return pltpu.make_async_remote_copy(
            src_ref=src, dst_ref=dst, send_sem=send, recv_sem=recv,
            device_id=device, device_id_type=MESH,
        )

    barrier = pltpu.get_barrier_semaphore()
    for neighbour in (up, down):
        pl.semaphore_signal(barrier, inc=1, device_id={"section": neighbour}, device_id_type=MESH)

    def place(k):
        to = (me + k + 1) % (R * C)
        return to, {"row": to // C, "col": to % C}

    def greet(k):
        pl.semaphore_signal(barrier, inc=1, device_id=place(k)[1], device_id_type=MESH)

    each(R * C - 1, greet)

    @pl.when(even)
    def _():
        local(act_in.at[0], lead.at[r], 0).start()
        local(grad_in.at[0], other, 1).start()

    @pl.when(odd)
    def _():
        local(grad_in.at[0], lead.at[r], 0).start()
        local(act_in.at[0], other, 1).start()

    local_saved = local(saved_in.at[0], saved, 2)
    local_hid, local_pre = local(hid_in.at[0], hid, 3), local(pre_in.at[0], pre, 4)
    local_gain, local_bias = local(gain_in, gain, 5), local(bias_in, bias, 6)
    for copy in (local_saved, local_hid, local_pre):
        copy.start()

    def weight_copy(i):
        rows = pl.ds(i * K, K)
        return pltpu.make_async_copy(weights.at[0, rows], w.at[rows], w_sem.at[i])

    for i in range(N):
        weight_copy(i).start()
    local_gain.start()
    local_bias.start()

    pl.semaphore_wait(barrier, R * C + 1)

    def lead_copy(src, to):
        return remote(src, lead.at[r], lead_send.at[to], lead_recv.at[r], row=to)

    @pl.when(even)
    def _():
        each(R - 1, lambda k: lead_copy(act_in.at[0], (r + k + 1) % R).start())

    @pl.when(odd)
    def _():
        each(R - 1, lambda k: lead_copy(grad_in.at[0], (r + k + 1) % R).start())

    def stat_copy(k):
        to, device = place(k)
        return remote(stats.at[me], stats.at[me], stat_send.at[to], stat_recv.at[me], **device)

    local(act_in.at[0], lead.at[r], 0).wait()
    local_saved.wait()

    @pl.when(even)
    def _():
        v = lead[r].astype(jnp.float32)
        z = saved[...].astype(jnp.float32)
        stats[me, 0] = row_sum(v)
        stats[me, 1] = row_sum(v * v)
        stats[me, 2] = row_sum(z)
        stats[me, 3] = row_sum(z * z)
        each(R * C - 1, lambda k: stat_copy(k).start())

    local_hid.wait()
    local_pre.wait()

    def act_edge(src, k):
        return remote(src, act_out.at[0], edge_send.at[k], edge_recv.at[0], section=up)

    def grad_edge(src, k):
        return remote(src, grad_out.at[0], edge_send.at[k], edge_recv.at[1], section=down)

    cut = F // 256 * 256
    pack = F - cut == LANES and DC % 2048 == 0
    wide = DC // (N // 2)

    def spread(rows):
        right[...] = rows.astype(jnp.bfloat16)
        if pack:
            last, none = rows[:, cut:], jnp.zeros((T, LANES), jnp.float32)
            upper = jnp.concatenate([last, none], axis=1)
            lower = jnp.concatenate([none, last], axis=1)
            last_right[...] = jnp.concatenate([upper, lower], axis=0).astype(jnp.bfloat16)

    @pl.when(even)
    def _():
        act_edge(lead.at[r], 0).start()
        h = hid[...].astype(jnp.float32)
        spread(h * gelu_slope(pre[...].astype(jnp.float32)))

    @pl.when(odd)
    def _():
        grad_edge(lead.at[r], 0).start()
        spread(hid[...].astype(jnp.float32))

    G = N // 2

    def part_copy(i, to):
        columns = pl.ds(i * wide, wide)
        return remote(
            parts.at[to, :, columns], sums.at[r, :, columns],
            part_send.at[i, to], part_recv.at[i, r], row=to,
        )

    def across(a, b):
        return lax.dot_general(
            a, b, (((1,), (1,)), ((), ())), preferred_element_type=jnp.float32
        )

    for i in range(G):
        weight_copy(2 * i).wait()
        weight_copy(2 * i + 1).wait()
        low, high = i * wide, (i + 1) * wide
        middle = low + wide // 2
        if pack:
            beside = jnp.concatenate([w[low:middle, cut:], w[middle:high, cut:]], axis=1)
            both = across(last_right[...], beside)
            term = across(right[:, :cut], w[low:high, :cut])
            term = term + jnp.concatenate([both[:T], both[T:]], axis=1)
        else:
            term = across(right[...], w[low:high, :])
        for q in range(R):
            parts[q, :, low:high] = term[q * own:(q + 1) * own, :]
        each(R - 1, lambda k: part_copy(i, (r + k + 1) % R).start())

    def lead_arrived(k):
        q = (r + k + 1) % R
        remote(lead.at[q], lead.at[q], lead_send.at[q], lead_recv.at[q], row=q).wait_recv()

    each(R - 1, lead_arrived)

    def stat_arrived(k):
        q, device = place(k)
        remote(stats.at[q], stats.at[q], stat_send.at[q], stat_recv.at[q], **device).wait_recv()

    def factors(q, first):
        total, squares = stats[q * C, first], stats[q * C, first + 1]
        for j in range(1, C):
            total = total + stats[q * C + j, first]
            squares = squares + stats[q * C + j, first + 1]
        average = total / D
        return average, lax.rsqrt(squares / D - average * average + EPSILON)

    @pl.when(even)
    def _():
        each(R * C - 1, stat_arrived)
        for q in range(R):
            rows = slice(q * own, (q + 1) * own)
            average, inverse = factors(q, 0)
            mean[rows, :] = average
            scale[rows, :] = inverse

    for q in range(R):
        x[q * own:(q + 1) * own, :] = lead[q].astype(jnp.float32)

    local(act_in.at[0], other, 1).wait()
    local_gain.wait()
    local_bias.wait()

    def dot(a, b):
        return jnp.dot(a.astype(jnp.bfloat16), b, preferred_element_type=jnp.float32)

    def portion(first, count):
        quarter = DC // 4
        base, span = first * quarter, count * quarter

        def product(left):
            if not pack:
                return dot(left, w[base:base + span, :])
            middle = span // 2
            sums_of = [0.0, 0.0, 0.0]
            for at in range(0, middle, 256):
                low, high = left[:, at:at + 256], left[:, middle + at:middle + at + 256]
                w_low = w[base + at:base + at + 256, :]
                w_high = w[base + middle + at:base + middle + at + 256, :]
                beside = jnp.concatenate([w_low[:, cut:], w_high[:, cut:]], axis=1)
                stacked = jnp.concatenate([low, high], axis=0)
                terms = dot(low, w_low[:, :cut]), dot(high, w_high[:, :cut]), dot(stacked, beside)
                sums_of = [kept + term for kept, term in zip(sums_of, terms)]
            main, both = sums_of[0] + sums_of[1], sums_of[2]
            return jnp.concatenate([main, both[:T, :LANES] + both[T:, LANES:]], axis=1)

        def keep(total):
            partial[c] = total if first == 0 else partial[c] + total

        columns = slice(base, base + span)

        @pl.when(even)
        def _():
            m, f = mean[:, :1], scale[:, :1]

            g, b = gain[pl.ds(layer, 1), columns], bias[pl.ds(layer, 1), columns]
            keep(product((x[:, columns] - m) * f * g + b))

        @pl.when(odd)
        def _():
            keep(product(x[:, columns]))

    portion(0, 2)

    def col_copy(k):
        to = (c + k + 1) % C
        return remote(partial.at[c], partial.at[c], col_send.at[to], col_recv.at[c], col=to)

    def part_arrived(k):
        q = (r + k + 1) % R
        for i in range(G):
            columns = pl.ds(i * wide, wide)
            remote(
                parts.at[q, :, columns], sums.at[q, :, columns],
                part_send.at[i, q], part_recv.at[i, q], row=q,
            ).wait_recv()

    each(R - 1, part_arrived)
    sums[r] = parts[r]
    term = sums[0]
    for q in range(1, R):
        term = term + sums[q]

    @pl.when(odd)
    def _():
        result[...] = (other[...].astype(jnp.float32) + term).astype(jnp.bfloat16)
        act_edge(result, 1).start()

    def mom_copy(k):
        to = (c + k + 1) % C
        return remote(moments.at[c], moments.at[c], mom_send.at[to], mom_recv.at[c], col=to)

    def saved_hat():
        average, inverse = factors(r, 2)
        return (saved[...].astype(jnp.float32) - average[:, :1]) * inverse[:, :1], inverse[:, :1]

    @pl.when(even)
    def _():
        scaled = term * gain[pl.ds(layer, 1), :]
        sums[0] = scaled
        moments[c, 0] = row_sum(scaled)
        moments[c, 1] = row_sum(scaled * saved_hat()[0])
        each(C - 1, lambda k: mom_copy(k).start())

    portion(2, 1)

    @pl.when(even)
    def _():
        def mom_arrived(k):
            q = (c + k + 1) % C
            remote(moments.at[q], moments.at[q], mom_send.at[q], mom_recv.at[q], col=q).wait_recv()

        each(C - 1, mom_arrived)
        first, second = moments[0, 0], moments[0, 1]
        for q in range(1, C):
            first = first + moments[q, 0]
            second = second + moments[q, 1]
        first, second = first[:, :1] / D, second[:, :1] / D
        h, inverse = saved_hat()
        moved = other[...].astype(jnp.float32) + inverse * (sums[0] - first - h * second)
        result[...] = moved.astype(jnp.bfloat16)
        grad_edge(result, 1).start()

    portion(3, 1)
    each(C - 1, lambda k: col_copy(k).start())

    def col_arrived(k):
        q = (c + k + 1) % C
        remote(partial.at[q], partial.at[q], col_send.at[q], col_recv.at[q], col=q).wait_recv()

    each(C - 1, col_arrived)
    summed = partial[0]
    for q in range(1, C):
        summed = summed + partial[q]

    @pl.when(even)
    def _():
        hidden[...] = gelu(summed).astype(jnp.bfloat16)

    @pl.when(odd)
    def _():
        hidden[...] = summed.astype(jnp.bfloat16)

    pair = s + 1 - 2 * (s % 2)
    hid_copy = remote(hidden, hid_out.at[0], edge_send.at[2], edge_recv.at[2], section=pair)
    hid_copy.start()

    act_edge(result, 0).wait_recv()
    grad_edge(result, 0).wait_recv()
    hid_copy.wait()
    for k in range(2):
        act_edge(result, k).wait_send()
    each(R - 1, lambda k: lead_copy(lead.at[r], (r + k + 1) % R).wait_send())
    for i in range(G):
        each(R - 1, lambda k: part_copy(i, (r + k + 1) % R).wait_send())
    each(C - 1, lambda k: col_copy(k).wait_send())

    @pl.when(even)
    def _():
        each(R * C - 1, lambda k: stat_copy(k).wait_send())
        each(C - 1, lambda k: mom_copy(k).wait_send())


def write_out(a, b, c, a_out, b_out, c_out, sem):
    pairs = ((a, a_out), (b, b_out), (c, c_out))
    copies = [pltpu.make_async_copy(i, o, sem.at[k]) for k, (i, o) in enumerate(pairs)]
    for copy in copies:
        copy.start()
    for copy in copies:
        copy.wait()


def per_device(S, R, C, *arguments):
    act_in, hid_in, grad_in, saved_in, saved_pre, weights, norm_gain, norm_bias = arguments
    own, DC = act_in.shape[1:]
    T, F = hid_in.shape[1:]
    N = 8
    bf16, f32 = jnp.bfloat16, jnp.float32
    dma = pltpu.SemaphoreType.DMA
    scratch = [
        pltpu.VMEM((DC, F), bf16),
        pltpu.VMEM((R, own, DC), bf16),
        pltpu.VMEM((own, DC), bf16),
        pltpu.VMEM((own, DC), bf16),
        pltpu.VMEM((T, F), bf16),
        pltpu.VMEM((T, F), bf16),
        pltpu.VMEM(norm_gain.shape, f32),
        pltpu.VMEM(norm_bias.shape, f32),
        pltpu.VMEM((T, F), bf16),
        pltpu.VMEM((2 * T, 2 * LANES), bf16),
        pltpu.VMEM((T, DC), f32),
        pltpu.VMEM((T, LANES), f32),
        pltpu.VMEM((T, LANES), f32),
        pltpu.VMEM((R * C, 4, own, LANES), f32),
        pltpu.VMEM((R, own, DC), f32),
        pltpu.VMEM((R, own, DC), f32),
        pltpu.VMEM((C, T, F), f32),
        pltpu.VMEM((C, 2, own, LANES), f32),
        pltpu.VMEM((T, F), bf16),
        pltpu.VMEM((own, DC), bf16),
        dma((N,)), dma((7,)),
        dma((R,)), dma((R,)),
        dma((R * C,)), dma((R * C,)),
        dma((N // 2, R)), dma((N // 2, R)),
        dma((C,)), dma((C,)),
        dma((C,)), dma((C,)),
        dma((3,)), dma((3,)),
    ]
    flops = 4 * T * F * DC
    moved = 2 * DC * F
    results = pl.pallas_call(
        functools.partial(kernel, (S, R, C, own, T, F, DC, N)),
        out_shape=[
            pltpu.VMEM(act_in.shape, bf16),
            pltpu.VMEM(hid_in.shape, bf16),
            pltpu.VMEM(grad_in.shape, bf16),
        ],
        in_specs=[pl.BlockSpec(memory_space=pl.ANY)] * 8,
        out_specs=[pl.BlockSpec(memory_space=pl.ANY)] * 3,
        scratch_shapes=scratch,
        compiler_params=pltpu.CompilerParams(
            collective_id=0, has_side_effects=True, vmem_limit_bytes=LIMIT
        ),
        cost_estimate=pl.CostEstimate(flops=flops, bytes_accessed=moved, transcendentals=T * F),
    )(*(pltpu.with_memory_space_constraint(a, pltpu.HBM) for a in arguments))
    return pl.pallas_call(
        write_out,
        out_shape=[jax.ShapeDtypeStruct(a.shape, a.dtype) for a in results],
        in_specs=[pl.BlockSpec(memory_space=pl.ANY)] * 3,
        out_specs=[pl.BlockSpec(memory_space=pl.ANY)] * 3,
        scratch_shapes=[dma((3,))],
        compiler_params=pltpu.CompilerParams(vmem_limit_bytes=LIMIT),
    )(*results)


def solution(mesh):
    S, R, C = (mesh.shape[name] for name in ("section", "row", "col"))
    in_specs = (
        P("section", "row", "col"),
        P("section", None, "row"),
        P("section", "row", "col"),
        P("section", "row", "col"),
        P("section", None, "row"),
        P("section", "col", "row"),
        P(None, "col"),
        P(None, "col"),
    )
    out_specs = (P("section", "row", "col"), P("section", None, "row"), P("section", "row", "col"))
    return jax.shard_map(
        functools.partial(per_device, S, R, C),
        mesh=mesh, in_specs=in_specs, out_specs=out_specs, check_vma=False,
    )
```

```python
import functools

import jax
import jax.numpy as jnp
from jax import lax
from jax.experimental import pallas as pl
from jax.experimental.pallas import tpu as pltpu
from jax.sharding import PartitionSpec as P

EPSILON = 1e-05
ROOT = 0.7978845608028654
CUBIC = 0.044715
MESH = pl.DeviceIdType.MESH
LANES = 128
LIMIT = 48 * 2**20


def each(count, body):
    if count <= 8:
        for step in range(count):
            body(step)
    else:
        lax.fori_loop(0, count, lambda step, carry: (body(step), carry)[1], 0)


def gelu(x):
    return x * (0.5 * (1.0 + jnp.tanh(ROOT * (x + CUBIC * (x * x * x)))))


def gelu_slope(x):
    t = jnp.tanh(ROOT * (x + CUBIC * (x * x * x)))
    return 0.5 * (1.0 + t) + 0.5 * x * (1.0 - t * t) * (ROOT * (1.0 + 3.0 * CUBIC * (x * x)))


def row_sum(values):
    return jnp.broadcast_to(jnp.sum(values, axis=-1, keepdims=True), (values.shape[0], LANES))


def kernel(
    sizes,
    act_in, hid_in, grad_in, saved_in, pre_in, weights, gain_in, bias_in,
    act_out, hid_out, grad_out,
    w, lead, other, saved, hid, pre, gain, bias, right, last_right, x, mean, scale, stats,
    parts, sums, partial, moments, hidden, result,
    w_sem, local_sem, lead_send, lead_recv, stat_send, stat_recv, part_send, part_recv,
    col_send, col_recv, mom_send, mom_recv, edge_send, edge_recv,
):
    S, R, C, own, T, F, DC, N = sizes
    D = DC * C
    K = DC // N
    s, r, c = lax.axis_index("section"), lax.axis_index("row"), lax.axis_index("col")
    even = s % 2 == 0
    odd = s % 2 == 1
    layer = s // 2
    up, down = (s + 1) % S, (s + S - 1) % S
    me = r * C + c

    def local(src, dst, k):
        return pltpu.make_async_copy(src, dst, local_sem.at[k])

    def remote(src, dst, send, recv, **device):
        return pltpu.make_async_remote_copy(
            src_ref=src, dst_ref=dst, send_sem=send, recv_sem=recv,
            device_id=device, device_id_type=MESH,
        )

    local_hid, local_pre = local(hid_in.at[0], hid, 3), local(pre_in.at[0], pre, 4)
    local_hid.start()
    local_pre.start()

    def weight_copy(i):
        rows = pl.ds(i * K, K)
        return pltpu.make_async_copy(weights.at[0, rows], w.at[rows], w_sem.at[i])

    for i in range(N):
        weight_copy(i).start()

    barrier = pltpu.get_barrier_semaphore()
    for neighbour in (up, down):
        pl.semaphore_signal(barrier, inc=1, device_id={"section": neighbour}, device_id_type=MESH)

    def place(k):
        to = (me + k + 1) % (R * C)
        return to, {"row": to // C, "col": to % C}

    def greet(k):
        pl.semaphore_signal(barrier, inc=1, device_id=place(k)[1], device_id_type=MESH)

    each(R * C - 1, greet)

    @pl.when(even)
    def _():
        local(act_in.at[0], lead.at[r], 0).start()
        local(grad_in.at[0], other, 1).start()

    @pl.when(odd)
    def _():
        local(grad_in.at[0], lead.at[r], 0).start()
        local(act_in.at[0], other, 1).start()

    local_saved = local(saved_in.at[0], saved, 2)
    local_gain, local_bias = local(gain_in, gain, 5), local(bias_in, bias, 6)
    local_saved.start()
    local_gain.start()
    local_bias.start()

    pl.semaphore_wait(barrier, R * C + 1)

    def lead_copy(src, to):
        return remote(src, lead.at[r], lead_send.at[to], lead_recv.at[r], row=to)

    @pl.when(even)
    def _():
        each(R - 1, lambda k: lead_copy(act_in.at[0], (r + k + 1) % R).start())

    @pl.when(odd)
    def _():
        each(R - 1, lambda k: lead_copy(grad_in.at[0], (r + k + 1) % R).start())

    def stat_copy(k):
        to, device = place(k)
        return remote(stats.at[me], stats.at[me], stat_send.at[to], stat_recv.at[me], **device)

    local(act_in.at[0], lead.at[r], 0).wait()
    local_saved.wait()

    @pl.when(even)
    def _():
        v = lead[r].astype(jnp.float32)
        z = saved[...].astype(jnp.float32)
        stats[me, 0] = row_sum(v)
        stats[me, 1] = row_sum(v * v)
        stats[me, 2] = row_sum(z)
        stats[me, 3] = row_sum(z * z)
        each(R * C - 1, lambda k: stat_copy(k).start())

    local_hid.wait()
    local_pre.wait()

    def act_edge(src, k):
        return remote(src, act_out.at[0], edge_send.at[k], edge_recv.at[0], section=up)

    def grad_edge(src, k):
        return remote(src, grad_out.at[0], edge_send.at[k], edge_recv.at[1], section=down)

    cut = F // 256 * 256
    pack = F - cut == LANES and DC % 2048 == 0
    wide = DC // (N // 2)

    def spread(rows):
        right[...] = rows.astype(jnp.bfloat16)
        if pack:
            last, none = rows[:, cut:], jnp.zeros((T, LANES), jnp.float32)
            upper = jnp.concatenate([last, none], axis=1)
            lower = jnp.concatenate([none, last], axis=1)
            last_right[...] = jnp.concatenate([upper, lower], axis=0).astype(jnp.bfloat16)

    @pl.when(even)
    def _():
        act_edge(lead.at[r], 0).start()
        h = hid[...].astype(jnp.float32)
        spread(h * gelu_slope(pre[...].astype(jnp.float32)))

    @pl.when(odd)
    def _():
        grad_edge(lead.at[r], 0).start()
        spread(hid[...].astype(jnp.float32))

    G = N // 2

    def part_copy(i, to):
        columns = pl.ds(i * wide, wide)
        return remote(
            parts.at[to, :, columns], sums.at[r, :, columns],
            part_send.at[i, to], part_recv.at[i, r], row=to,
        )

    def across(a, b):
        return lax.dot_general(
            a, b, (((1,), (1,)), ((), ())), preferred_element_type=jnp.float32
        )

    for i in range(G):
        weight_copy(2 * i).wait()
        weight_copy(2 * i + 1).wait()
        low, high = i * wide, (i + 1) * wide
        middle = low + wide // 2
        if pack:
            beside = jnp.concatenate([w[low:middle, cut:], w[middle:high, cut:]], axis=1)
            both = across(last_right[...], beside)
            term = across(right[:, :cut], w[low:high, :cut])
            term = term + jnp.concatenate([both[:T], both[T:]], axis=1)
        else:
            term = across(right[...], w[low:high, :])
        for q in range(R):
            parts[q, :, low:high] = term[q * own:(q + 1) * own, :]
        each(R - 1, lambda k: part_copy(i, (r + k + 1) % R).start())

    def lead_arrived(k):
        q = (r + k + 1) % R
        remote(lead.at[q], lead.at[q], lead_send.at[q], lead_recv.at[q], row=q).wait_recv()

    each(R - 1, lead_arrived)

    def stat_arrived(k):
        q, device = place(k)
        remote(stats.at[q], stats.at[q], stat_send.at[q], stat_recv.at[q], **device).wait_recv()

    def factors(q, first):
        total, squares = stats[q * C, first], stats[q * C, first + 1]
        for j in range(1, C):
            total = total + stats[q * C + j, first]
            squares = squares + stats[q * C + j, first + 1]
        average = total / D
        return average, lax.rsqrt(squares / D - average * average + EPSILON)

    @pl.when(even)
    def _():
        each(R * C - 1, stat_arrived)
        for q in range(R):
            rows = slice(q * own, (q + 1) * own)
            average, inverse = factors(q, 0)
            mean[rows, :] = average
            scale[rows, :] = inverse

    for q in range(R):
        x[q * own:(q + 1) * own, :] = lead[q].astype(jnp.float32)

    local(act_in.at[0], other, 1).wait()
    local_gain.wait()
    local_bias.wait()

    def dot(a, b):
        return jnp.dot(a.astype(jnp.bfloat16), b, preferred_element_type=jnp.float32)

    def portion(first, count):
        quarter = DC // 4
        base, span = first * quarter, count * quarter

        def product(left):
            if not pack:
                return dot(left, w[base:base + span, :])
            main = dot(left, w[base:base + span, :cut])
            middle = span // 2
            stacked = jnp.concatenate([left[:, :middle], left[:, middle:]], axis=0)
            beside = jnp.concatenate(
                [w[base:base + middle, cut:], w[base + middle:base + span, cut:]], axis=1
            )
            both = dot(stacked, beside)
            return jnp.concatenate([main, both[:T, :LANES] + both[T:, LANES:]], axis=1)

        def keep(total):
            partial[c] = total if first == 0 else partial[c] + total

        columns = slice(base, base + span)

        @pl.when(even)
        def _():
            m, f = mean[:, :1], scale[:, :1]

            g, b = gain[pl.ds(layer, 1), columns], bias[pl.ds(layer, 1), columns]
            keep(product((x[:, columns] - m) * f * g + b))

        @pl.when(odd)
        def _():
            keep(product(x[:, columns]))

    portion(0, 3)

    def col_copy(k):
        to = (c + k + 1) % C
        return remote(partial.at[c], partial.at[c], col_send.at[to], col_recv.at[c], col=to)

    def part_arrived(k):
        q = (r + k + 1) % R
        for i in range(G):
            columns = pl.ds(i * wide, wide)
            remote(
                parts.at[q, :, columns], sums.at[q, :, columns],
                part_send.at[i, q], part_recv.at[i, q], row=q,
            ).wait_recv()

    each(R - 1, part_arrived)
    sums[r] = parts[r]
    term = sums[0]
    for q in range(1, R):
        term = term + sums[q]

    @pl.when(odd)
    def _():
        result[...] = (other[...].astype(jnp.float32) + term).astype(jnp.bfloat16)
        act_edge(result, 1).start()

    def mom_copy(k):
        to = (c + k + 1) % C
        return remote(moments.at[c], moments.at[c], mom_send.at[to], mom_recv.at[c], col=to)

    def saved_hat():
        average, inverse = factors(r, 2)
        return (saved[...].astype(jnp.float32) - average[:, :1]) * inverse[:, :1], inverse[:, :1]

    @pl.when(even)
    def _():
        scaled = term * gain[pl.ds(layer, 1), :]
        sums[0] = scaled
        moments[c, 0] = row_sum(scaled)
        moments[c, 1] = row_sum(scaled * saved_hat()[0])
        each(C - 1, lambda k: mom_copy(k).start())

    portion(3, 1)
    each(C - 1, lambda k: col_copy(k).start())

    @pl.when(even)
    def _():
        def mom_arrived(k):
            q = (c + k + 1) % C
            remote(moments.at[q], moments.at[q], mom_send.at[q], mom_recv.at[q], col=q).wait_recv()

        each(C - 1, mom_arrived)
        first, second = moments[0, 0], moments[0, 1]
        for q in range(1, C):
            first = first + moments[q, 0]
            second = second + moments[q, 1]
        first, second = first[:, :1] / D, second[:, :1] / D
        h, inverse = saved_hat()
        moved = other[...].astype(jnp.float32) + inverse * (sums[0] - first - h * second)
        result[...] = moved.astype(jnp.bfloat16)
        grad_edge(result, 1).start()

    def col_arrived(k):
        q = (c + k + 1) % C
        remote(partial.at[q], partial.at[q], col_send.at[q], col_recv.at[q], col=q).wait_recv()

    each(C - 1, col_arrived)
    summed = partial[0]
    for q in range(1, C):
        summed = summed + partial[q]

    @pl.when(even)
    def _():
        hidden[...] = gelu(summed).astype(jnp.bfloat16)

    @pl.when(odd)
    def _():
        hidden[...] = summed.astype(jnp.bfloat16)

    pair = s + 1 - 2 * (s % 2)
    hid_copy = remote(hidden, hid_out.at[0], edge_send.at[2], edge_recv.at[2], section=pair)
    hid_copy.start()

    act_edge(result, 0).wait_recv()
    grad_edge(result, 0).wait_recv()
    hid_copy.wait()
    for k in range(2):
        act_edge(result, k).wait_send()
    each(R - 1, lambda k: lead_copy(lead.at[r], (r + k + 1) % R).wait_send())
    for i in range(G):
        each(R - 1, lambda k: part_copy(i, (r + k + 1) % R).wait_send())
    each(C - 1, lambda k: col_copy(k).wait_send())

    @pl.when(even)
    def _():
        each(R * C - 1, lambda k: stat_copy(k).wait_send())
        each(C - 1, lambda k: mom_copy(k).wait_send())


def write_out(a, b, c, a_out, b_out, c_out, sem):
    pairs = ((a, a_out), (b, b_out), (c, c_out))
    copies = [pltpu.make_async_copy(i, o, sem.at[k]) for k, (i, o) in enumerate(pairs)]
    for copy in copies:
        copy.start()
    for copy in copies:
        copy.wait()


def per_device(S, R, C, *arguments):
    act_in, hid_in, grad_in, saved_in, saved_pre, weights, norm_gain, norm_bias = arguments
    own, DC = act_in.shape[1:]
    T, F = hid_in.shape[1:]
    N = 8
    bf16, f32 = jnp.bfloat16, jnp.float32
    dma = pltpu.SemaphoreType.DMA
    scratch = [
        pltpu.VMEM((DC, F), bf16),
        pltpu.VMEM((R, own, DC), bf16),
        pltpu.VMEM((own, DC), bf16),
        pltpu.VMEM((own, DC), bf16),
        pltpu.VMEM((T, F), bf16),
        pltpu.VMEM((T, F), bf16),
        pltpu.VMEM(norm_gain.shape, f32),
        pltpu.VMEM(norm_bias.shape, f32),
        pltpu.VMEM((T, F), bf16),
        pltpu.VMEM((2 * T, 2 * LANES), bf16),
        pltpu.VMEM((T, DC), f32),
        pltpu.VMEM((T, LANES), f32),
        pltpu.VMEM((T, LANES), f32),
        pltpu.VMEM((R * C, 4, own, LANES), f32),
        pltpu.VMEM((R, own, DC), f32),
        pltpu.VMEM((R, own, DC), f32),
        pltpu.VMEM((C, T, F), f32),
        pltpu.VMEM((C, 2, own, LANES), f32),
        pltpu.VMEM((T, F), bf16),
        pltpu.VMEM((own, DC), bf16),
        dma((N,)), dma((7,)),
        dma((R,)), dma((R,)),
        dma((R * C,)), dma((R * C,)),
        dma((N // 2, R)), dma((N // 2, R)),
        dma((C,)), dma((C,)),
        dma((C,)), dma((C,)),
        dma((3,)), dma((3,)),
    ]
    flops = 4 * T * F * DC
    moved = 2 * DC * F
    results = pl.pallas_call(
        functools.partial(kernel, (S, R, C, own, T, F, DC, N)),
        out_shape=[
            pltpu.VMEM(act_in.shape, bf16),
            pltpu.VMEM(hid_in.shape, bf16),
            pltpu.VMEM(grad_in.shape, bf16),
        ],
        in_specs=[pl.BlockSpec(memory_space=pl.ANY)] * 8,
        out_specs=[pl.BlockSpec(memory_space=pl.ANY)] * 3,
        scratch_shapes=scratch,
        compiler_params=pltpu.CompilerParams(
            collective_id=0, has_side_effects=True, vmem_limit_bytes=LIMIT
        ),
        cost_estimate=pl.CostEstimate(flops=flops, bytes_accessed=moved, transcendentals=T * F),
    )(*(pltpu.with_memory_space_constraint(a, pltpu.HBM) for a in arguments))
    return pl.pallas_call(
        write_out,
        out_shape=[jax.ShapeDtypeStruct(a.shape, a.dtype) for a in results],
        in_specs=[pl.BlockSpec(memory_space=pl.ANY)] * 3,
        out_specs=[pl.BlockSpec(memory_space=pl.ANY)] * 3,
        scratch_shapes=[dma((3,))],
        compiler_params=pltpu.CompilerParams(vmem_limit_bytes=LIMIT),
    )(*results)


def solution(mesh):
    S, R, C = (mesh.shape[name] for name in ("section", "row", "col"))
    in_specs = (
        P("section", "row", "col"),
        P("section", None, "row"),
        P("section", "row", "col"),
        P("section", "row", "col"),
        P("section", None, "row"),
        P("section", "col", "row"),
        P(None, "col"),
        P(None, "col"),
    )
    out_specs = (P("section", "row", "col"), P("section", None, "row"), P("section", "row", "col"))
    return jax.shard_map(
        functools.partial(per_device, S, R, C),
        mesh=mesh, in_specs=in_specs, out_specs=out_specs, check_vma=False,
    )
```
